32 devices in a mesh: grp: 2 (over x), aux: 16 (over z, y, core).
Axes of the slice: x: 2, y: 2, z: 4, core: 2. Of those that a mesh axis runs over, the one named last changes fastest.
Arguments:
- raw_tiles: bfloat16 [32, 32, 32, 6, 128], P(('grp', 'aux')), parts along dimension 0, may hold values from -1.25 to 1.25
- metric: bfloat16 [32, 16], P('grp'), parts along dimension 0, may hold values from -2 to 2
- owner_map: int32 [64], P('grp'), parts along dimension 0, may hold values from 0 to 31, as said below
- counts: int32 [64], P(('grp', 'aux')), parts along dimension 0, may hold values from 1 to 5, as said below
Outputs:
- exchange_blocks: float32 [64, 768, 768], P(('grp', 'aux')), parts along dimension 0
The draws below stay inside these ranges and needn't reach their ends.
There are 2 independent parts, one for each index of `grp`. The reference program is written for one: setup_inputs(seed, part) draws one part's arguments, and reference() takes and returns one part's arrays. A program takes and returns all parts, laid end to end along the dimension named above; each array names one. Nothing has to cross between parts.
Inputs may be any that keep to these rules, and one draw needn't show every extreme that they name: Slots at or beyond counts[o] are ignored; for every d, the two blocks whose positions are 2 d and 2 d + 1 have counts summing to at most 6, and some such pair reaches 6; 5 is reached by some block. `owner_map`: every position 0 to 31 once.
All inputs are finite; a program needn't handle non-finite values.
Results may differ from the reference program's by a relative error of at most 0.0027.
Values may be sent and summed in bfloat16 or wider, within the bound.
No kernel may reach another device: no remote copies, remote signals or barrier semaphores. Data moves between devices by JAX's collectives and lax.ppermute only.
A program may use at most 64 MiB of HBM per device.

```python
import jax
import jax.numpy as jnp
from jax import lax

BS = 128
OB = 32
DOM = 6
AUX = 16
NOB = 32


def joint_draw(key):
    perm_key, first_key, second_key, full_key = jax.random.split(key, 4)
    owner = jax.random.permutation(perm_key, NOB).astype(jnp.int32)
    held = jnp.zeros((NOB,), jnp.int32).at[owner].set(jnp.arange(NOB, dtype=jnp.int32))
    pair_total = NOB // 2
    first = jax.random.randint(first_key, (pair_total,), 1, DOM).astype(jnp.int32)
    spare = DOM - first
    second = 1 + jax.random.randint(second_key, (pair_total,), 0, 1048576).astype(jnp.int32) % spare
    fullest = jax.random.randint(full_key, (), 0, pair_total)
    is_full = jnp.arange(pair_total) == fullest
    first = jnp.where(is_full, DOM - 1, first)
    second = jnp.where(is_full, 1, second)
    per_position = jnp.stack([first, second], axis=1).reshape(-1).astype(jnp.int32)
    counts_out = jnp.zeros((NOB,), jnp.int32).at[held].set(per_position)
    return (owner, counts_out)


def draw_owner_map(key, part):
    return joint_draw(key)[0]


def draw_counts(key, part):
    return joint_draw(key)[1]


def draw_metric(key, part):
    key = jax.random.fold_in(key, 11)
    noise_field = jax.random.normal(key, (AUX, AUX), jnp.float32)
    symmetric = (noise_field + noise_field.T) * (0.35 / (2.0 * AUX) ** 0.5)
    return (symmetric + jnp.eye(AUX, dtype=jnp.float32)).astype(jnp.bfloat16)


def shard_levels(stream_key, dims, cuts, least, high):
    factor_of = 1.0
    for axis_at, blocks in cuts:
        heights = jax.random.uniform(jax.random.fold_in(jax.random.fold_in(stream_key, 6), axis_at), (blocks,), jnp.float32, least / len(cuts), high / len(cuts))
        factor_of = factor_of * jnp.repeat(jnp.exp(heights), dims[axis_at] // blocks).reshape((-1,) + (1,) * (len(dims) - 1 - axis_at))
    return factor_of


def gaussian(key, dims, spread, most, cuts=(), kind=jnp.bfloat16):
    drawn = jax.random.normal(key, dims, jnp.float32) * spread
    if len(cuts) > 0:
        drawn = shard_levels(key, dims, cuts, -0.22, 0.18) * drawn
    return jnp.clip(drawn, min=-most, max=most).astype(kind)


def setup_inputs(seed: int = 0, part: int = 0) -> dict:
    streams_of = jax.random.split(jax.random.key(seed), 5)
    part_splits = jax.random.split(jax.random.fold_in(streams_of[4], part), 5)
    return {
        "raw_tiles": gaussian(part_splits[0], (AUX, NOB, OB, DOM, BS), ((AUX * OB) ** -0.25), 1.25, ((0, 16),)),
        "metric": draw_metric(jax.random.fold_in(jax.random.fold_in(streams_of[4], part), 71), part),
        "owner_map": draw_owner_map(jax.random.fold_in(jax.random.fold_in(streams_of[4], part), 71), part),
        "counts": draw_counts(jax.random.fold_in(jax.random.fold_in(streams_of[4], part), 71), part),
    }


def one_block(raw_tiles, metric, counts, block_id):
    chosen = lax.dynamic_index_in_dim(raw_tiles, block_id, 1, keepdims=False)
    aux_total, orbitals, domain, tile_width = chosen.shape
    slot_ids = jnp.arange(domain, dtype=jnp.int32)
    live_slots = lax.dynamic_index_in_dim(counts, block_id, 0, keepdims=False)
    masked = jnp.where((slot_ids < live_slots)[None, None, :, None], chosen, jnp.zeros_like(chosen))
    fitted = jnp.dot(metric, masked.reshape(aux_total, orbitals * domain * tile_width), preferred_element_type=jnp.float32)
    fitted = fitted.astype(jnp.bfloat16).reshape(aux_total * orbitals, domain * tile_width)
    return jnp.dot(fitted.T, fitted, preferred_element_type=jnp.float32)


def reference(raw_tiles, metric, owner_map, counts):
    block_ids = jnp.arange(NOB, dtype=jnp.int32)
    blocks = lax.map(lambda block_id: one_block(raw_tiles, metric, counts, block_id), block_ids)
    return jnp.zeros_like(blocks).at[owner_map].set(blocks)
```

```python
import functools

import jax
import jax.numpy as jnp
from jax import lax
from jax.experimental import pallas as pl
from jax.experimental.pallas import tpu as pltpu
from jax.sharding import PartitionSpec as P

ANY = pl.BlockSpec(memory_space=pl.ANY)
SMEM = pl.BlockSpec(memory_space=pltpu.SMEM)


def pack_kernel(chips, owner_ref, mine_ref, side_ref, *refs):
    half = chips // 2
    own_raw, peer_raw = refs[2 * (half - 1) : 2 * half]
    got, swapped = refs[: half - 1], refs[half - 1 : 2 * half - 2]
    outs = refs[2 * half : 3 * half]
    info_ref = refs[3 * half]
    held, table, small_sem, sems = refs[3 * half + 1 :]
    blocks, slots = own_raw.shape[0], own_raw.shape[1]
    me = lax.axis_index("aux")
    chip, core = me // 2, lax.rem(me, 2)

    rows = [(mine_ref, 0), (side_ref, 1)]
    for k in range(1, half):
        rows += [(got[k - 1], 2 * k), (swapped[k - 1], 2 * k + 1)]
    for n, (ref, row) in enumerate(rows):
        pltpu.make_async_copy(ref, table.at[row], small_sem.at[n]).start()

    def place(o, carry):
        held[owner_ref[o]] = o
        return carry

    lax.fori_loop(0, blocks, place, 0)
    for n, (ref, row) in enumerate(rows):
        pltpu.make_async_copy(ref, table.at[row], small_sem.at[n]).wait()

    def live(block):
        m = lax.bitwise_xor(block // 4, chip)
        parity = jnp.where(m >= 2, lax.bitwise_xor(lax.rem(m, 2), core), lax.rem(m, 2))
        return table[(m // 2) * 2 + parity, lax.rem(block, 4)]

    def pair(dest):
        first, second = held[2 * dest], held[2 * dest + 1]
        return first, second, live(first)

    def send(dest, target, sem):
        first, second, count = pair(dest)
        for j in range(slots):
            from_first = j < count
            block = jnp.where(from_first, first, second)
            slot = jnp.where(from_first, j, slots - 1 - j)
            pltpu.make_async_copy(own_raw.at[block, slot], target.at[core, j], sem).start()
            pltpu.make_async_copy(peer_raw.at[block, slot], target.at[1 - core, j], sem).start()

    for k in range(half - 1, 0, -1):
        there = lax.bitwise_xor(chip, 2 * k + core)
        for f in range(2):
            dest = 2 * there + (core if f == 0 else 1 - core)
            send(dest, outs[k].at[f], sems.at[k])
    send(2 * lax.bitwise_xor(chip, 1) + core, outs[0], sems.at[0])

    first, second, count = pair(me)
    info_ref[0] = first
    info_ref[1] = second
    info_ref[2] = count
    info_ref[3] = live(second)
    for k in range(half):
        pltpu.make_async_copy(outs[k], outs[k], sems.at[k]).wait()


def exchange_kernel(chips, info_ref, metric_ref, *refs):
    half = chips // 2
    own_raw, peer_raw, side = refs[:3]
    got, swapped = refs[3 : half + 2], refs[half + 2 : 2 * half + 1]
    out_ref, gathered, rows, stage, in_sems, out_sems = refs[2 * half + 1 :]
    aux, slots, orbitals, width = gathered.shape
    me = lax.axis_index("aux")
    chip, core = me // 2, lax.rem(me, 2)
    first, second, first_live, second_live = (info_ref[n] for n in range(4))

    def chip_rows(m):
        return gathered.at[pl.ds(2 * lax.bitwise_xor(chip, m), 2)]

    copies = [pltpu.make_async_copy(side, chip_rows(1), in_sems.at[0])]
    for k in range(1, half):
        copies.append(pltpu.make_async_copy(got[k - 1].at[0], chip_rows(2 * k + core), in_sems.at[2 * k]))
        copies.append(pltpu.make_async_copy(swapped[k - 1].at[1], chip_rows(2 * k + 1 - core), in_sems.at[2 * k + 1]))
    for copy in copies:
        copy.start()
    for j in range(slots):
        from_first = j < first_live
        block = jnp.where(from_first, first, second)
        slot = jnp.where(from_first, j, slots - 1 - j)
        pltpu.make_async_copy(own_raw.at[block, slot], gathered.at[2 * chip + core, j], in_sems.at[1]).start()
        pltpu.make_async_copy(peer_raw.at[block, slot], gathered.at[2 * chip + 1 - core, j], in_sems.at[1]).start()

    group = 16
    wide = aux * group
    pick = (lax.broadcasted_iota(jnp.int32, (wide, aux), 0) // group == lax.broadcasted_iota(jnp.int32, (wide, aux), 1)).astype(jnp.bfloat16)
    tall = jnp.dot(pick, metric_ref[...], preferred_element_type=jnp.float32).astype(jnp.bfloat16)
    spread = lax.dot_general(tall, pick, (((1,), (1,)), ((), ())), preferred_element_type=jnp.float32)
    same = lax.rem(lax.broadcasted_iota(jnp.int32, (wide, wide), 0), group) == lax.rem(lax.broadcasted_iota(jnp.int32, (wide, wide), 1), group)
    factor = jnp.where(same, spread, 0.0).astype(jnp.bfloat16)

    for copy in copies:
        copy.wait()
    pltpu.make_async_copy(chip_rows(0), chip_rows(0), in_sems.at[1]).wait()

    for part in range(orbitals // group):
        columns = [gathered[:, s, part * group : (part + 1) * group, :].reshape(wide, width) for s in range(slots)]
        fitted = jnp.dot(factor, jnp.concatenate(columns, axis=1), preferred_element_type=jnp.float32)
        rows[part * wide : (part + 1) * wide, :] = fitted.astype(jnp.bfloat16)

    def span(n):
        return slice(n * width, (n + 1) * width)

    for s in range(slots):
        product = lax.dot_general(rows[:, span(s)], rows[...], (((0,), (0,)), ((), ())), preferred_element_type=jnp.float32)
        for which, count in ((0, first_live), (1, second_live)):
            row = s if which == 0 else slots - 1 - s
            for t in range(slots):
                column = t if which == 0 else slots - 1 - t
                stage[which, span(row), span(column)] = jnp.where(max(row, column) < count, product[:, span(t)], 0.0)
            pltpu.make_async_copy(stage.at[which, span(row)], out_ref.at[which, span(row)], out_sems.at[which, row]).start()
    for which in range(2):
        for row in range(slots):
            pltpu.make_async_copy(stage.at[which, span(row)], out_ref.at[which, span(row)], out_sems.at[which, row]).wait()


def shards(devices, raw_tiles, metric, owner_map, counts):
    chips = devices // 2
    half = chips // 2
    _, blocks, orbitals, slots, width = raw_tiles.shape
    core = lax.rem(lax.axis_index("aux"), 2)
    raw = raw_tiles[0].transpose(0, 2, 1, 3)

    def swap(x):
        return lax.ppermute(x, "aux", [(i, i ^ 1) for i in range(devices)])

    def hop(x, k):
        def target(i):
            away = 1 if k == 0 else 2 * k + i % 2
            return (i // 2 ^ away) * 2 + i % 2

        return lax.ppermute(x, "aux", [(i, target(i)) for i in range(devices)])

    other = swap(counts)
    lane = lax.broadcasted_iota(jnp.int32, (128,), 0)
    mine = jnp.where(lane // 2 == core, jnp.where(lane % 2 == 0, counts[0], counts[1]), jnp.where(lane % 2 == 0, other[0], other[1]))
    peer_raw = swap(raw)
    got = [hop(mine, k) for k in range(half)]
    swapped = [swap(x) for x in got[1:]]

    packed = [jax.ShapeDtypeStruct((2, slots, orbitals, width), raw.dtype)]
    packed += [jax.ShapeDtypeStruct((2, 2, slots, orbitals, width), raw.dtype)] * (half - 1)
    *outgoing, info = pl.pallas_call(
        functools.partial(pack_kernel, chips),
        out_shape=packed + [jax.ShapeDtypeStruct((4,), jnp.int32)],
        in_specs=[SMEM] + [ANY] * (2 * half + 2),
        out_specs=[ANY] * half + [SMEM],
        scratch_shapes=[
            pltpu.SMEM((blocks,), jnp.int32),
            pltpu.SMEM((chips, 128), jnp.int32),
            pltpu.SemaphoreType.DMA((chips,)),
            pltpu.SemaphoreType.DMA((half,)),
        ],
        name="pack",
    )(owner_map, mine, got[0], *got[1:], *swapped, raw, peer_raw)

    arrived = [hop(x, k) for k, x in enumerate(outgoing)]
    crossed = [swap(x) for x in arrived[1:]]

    return pl.pallas_call(
        functools.partial(exchange_kernel, chips),
        out_shape=jax.ShapeDtypeStruct((2, slots * width, slots * width), jnp.float32),
        in_specs=[SMEM, pl.BlockSpec(memory_space=pltpu.VMEM)] + [ANY] * (2 * half + 1),
        out_specs=ANY,
        scratch_shapes=[
            pltpu.VMEM((devices, slots, orbitals, width), raw.dtype),
            pltpu.VMEM((devices * orbitals, slots * width), raw.dtype),
            pltpu.VMEM((2, slots * width, slots * width), jnp.float32),
            pltpu.SemaphoreType.DMA((chips,)),
            pltpu.SemaphoreType.DMA((2, slots)),
        ],
        compiler_params=pltpu.CompilerParams(vmem_limit_bytes=40 * 1024 * 1024),
        name="exchange",
    )(info, metric, raw, peer_raw, arrived[0], *arrived[1:], *crossed)


def solution(mesh):
    in_specs = (
        P(("grp", "aux"), None, None, None, None),
        P("grp", None),
        P("grp"),
        P(("grp", "aux")),
    )
    out_specs = P(("grp", "aux"), None, None)
    body = functools.partial(shards, mesh.shape["aux"])
    return jax.shard_map(body, mesh=mesh, in_specs=in_specs, out_specs=out_specs, check_vma=False)
```

```python
import functools

import jax
import jax.numpy as jnp
from jax import lax
from jax.experimental import pallas as pl
from jax.experimental.pallas import tpu as pltpu
from jax.sharding import PartitionSpec as P

VMEM = pl.BlockSpec(memory_space=pltpu.VMEM)
SMEM = pl.BlockSpec(memory_space=pltpu.SMEM)
GROUP = 16


def pack_kernel(chips, owner_ref, *refs):
    half = chips // 2
    rows = refs[:chips]
    own_raw, peer_raw = refs[chips : chips + 2]
    outs = refs[chips + 2 : chips + 2 + half]
    self_ref, info_ref, held, table, sems = refs[chips + 2 + half :]
    blocks, slots = own_raw.shape[0], own_raw.shape[1]
    me = lax.axis_index("aux")
    chip, core = me // 2, lax.rem(me, 2)

    copies = [pltpu.make_async_copy(ref, table.at[n], sems.at[n]) for n, ref in enumerate(rows)]
    for copy in copies:
        copy.start()

    def place(o, carry):
        held[owner_ref[o]] = o
        return carry

    lax.fori_loop(0, blocks, place, 0, unroll=True)
    for copy in copies:
        copy.wait()

    def live(block):
        m = lax.bitwise_xor(block // 4, chip)
        far = lax.bitwise_and(lax.bitwise_xor(m, core), 1)
        f = jnp.where(m >= 2, far, lax.bitwise_and(m, 1))
        sender = jnp.where(m >= 2, lax.bitwise_xor(core, far), core)
        lane = 2 * lax.bitwise_xor(lax.bitwise_and(block // 2, 1), sender) + lax.bitwise_and(block, 1)
        return table[(m // 2) * 2 + f, lane]

    def send(dest, target):
        first, second = held[2 * dest], held[2 * dest + 1]
        count = live(first)
        for j in range(slots):
            from_first = j < count
            block = jnp.where(from_first, first, second)
            slot = jnp.where(from_first, j, slots - 1 - j)
            target[core, j] = own_raw[block, slot]
            target[1 - core, j] = peer_raw[block, slot]
        return count, second

    for k in range(half - 1, 0, -1):
        there = lax.bitwise_xor(chip, 2 * k + core)
        for f in range(2):
            send(2 * there + (core if f == 0 else 1 - core), outs[k].at[f])
    send(2 * lax.bitwise_xor(chip, 1) + core, outs[0])
    count, second = send(me, self_ref)
    row = lax.broadcasted_iota(jnp.int32, info_ref.shape, 0)
    info_ref[...] = jnp.where(row == 0, count, live(second))


def factor_kernel(metric_ref, factor_ref):
    wide, aux = factor_ref.shape[0], metric_ref.shape[0]
    me = lax.axis_index("aux")
    chip, core = me // 2, lax.rem(me, 2)
    row = lax.broadcasted_iota(jnp.int32, (wide, aux), 0) // GROUP
    column = lax.broadcasted_iota(jnp.int32, (wide, aux), 1)
    pick = (row == column).astype(jnp.bfloat16)
    place = row // 2
    away = jnp.where(place < 2, place, lax.bitwise_xor(place, core))
    origin = 2 * lax.bitwise_xor(away, chip) + lax.bitwise_and(row, 1)
    pick_origin = (origin == column).astype(jnp.bfloat16)
    tall = jnp.dot(pick, metric_ref[...], preferred_element_type=jnp.float32).astype(jnp.bfloat16)
    spread = lax.dot_general(tall, pick_origin, (((1,), (1,)), ((), ())), preferred_element_type=jnp.float32)
    same = lax.rem(lax.broadcasted_iota(jnp.int32, (wide, wide), 0), GROUP) == lax.rem(
        lax.broadcasted_iota(jnp.int32, (wide, wide), 1), GROUP
    )
    factor_ref[...] = jnp.where(same, spread, 0.0).astype(jnp.bfloat16)


def exchange_kernel(chips, info_ref, factor_ref, self_ref, side_ref, *refs):
    half = chips // 2
    got, swapped = refs[: half - 1], refs[half - 1 : 2 * half - 2]
    out_ref, rows, stage, sems = refs[2 * half - 2 :]
    _, slots, orbitals, width = self_ref.shape
    wide = factor_ref.shape[0]
    arrivals = [self_ref, side_ref]
    for k in range(1, half):
        arrivals += [got[k - 1].at[0], swapped[k - 1].at[1]]

    def span(n):
        return slice(n * width, (n + 1) * width)

    for part in range(orbitals // GROUP):
        columns = [
            jnp.concatenate(
                [ref[q, s, part * GROUP : (part + 1) * GROUP, :] for ref in arrivals for q in range(2)], axis=0
            )
            for s in range(slots)
        ]
        fitted = jnp.dot(factor_ref[...], jnp.concatenate(columns, axis=1), preferred_element_type=jnp.float32)
        rows[part * wide : (part + 1) * wide, :] = fitted.astype(jnp.bfloat16)

    live = [info_ref[0:1, :], info_ref[1:2, :]]
    for s in range(slots):
        product = lax.dot_general(
            rows[:, span(s)], rows[...], (((0,), (0,)), ((), ())), preferred_element_type=jnp.float32
        )
        for which in range(2):
            row = s if which == 0 else slots - 1 - s
            for t in range(slots):
                column = t if which == 0 else slots - 1 - t
                stage[which, span(row), span(column)] = jnp.where(
                    live[which] > max(row, column), product[:, span(t)], 0.0
                )
            pltpu.make_async_copy(
                stage.at[which, span(row)], out_ref.at[which, span(row)], sems.at[which, row]
            ).start()
    for which in range(2):
        for row in range(slots):
            pltpu.make_async_copy(
                stage.at[which, span(row)], out_ref.at[which, span(row)], sems.at[which, row]
            ).wait()


def shards(devices, raw_tiles, metric, owner_map, counts):
    chips = devices // 2
    half = chips // 2
    _, _, orbitals, slots, width = raw_tiles.shape
    raw = raw_tiles[0].transpose(0, 2, 1, 3)

    def swap(x):
        return lax.ppermute(x, "aux", [(i, i ^ 1) for i in range(devices)])

    def hop(x, k):
        def target(i):
            away = 1 if k == 0 else 2 * k + i % 2
            return (i // 2 ^ away) * 2 + i % 2

        return lax.ppermute(x, "aux", [(i, target(i)) for i in range(devices)])

    other = swap(counts)
    mine = jnp.concatenate([counts, other, jnp.zeros((124,), jnp.int32)])
    raw, mine = lax.optimization_barrier((raw, mine))
    peer_raw = swap(raw)
    got = lax.optimization_barrier([hop(mine, k) for k in range(half)])
    rows = [mine, got[0]]
    for x in got[1:]:
        rows += [x, swap(x)]

    pair = jax.ShapeDtypeStruct((2, slots, orbitals, width), raw.dtype)
    pairs = jax.ShapeDtypeStruct((2, 2, slots, orbitals, width), raw.dtype)
    *outgoing, own, info = pl.pallas_call(
        functools.partial(pack_kernel, chips),
        out_shape=[pair] + [pairs] * (half - 1) + [pair, jax.ShapeDtypeStruct((8, 128), jnp.int32)],
        in_specs=[SMEM] + [VMEM] * (chips + 2),
        out_specs=[VMEM] * (half + 2),
        scratch_shapes=[
            pltpu.SMEM((raw.shape[0],), jnp.int32),
            pltpu.SMEM((chips, 128), jnp.int32),
            pltpu.SemaphoreType.DMA((chips,)),
        ],
        compiler_params=pltpu.CompilerParams(vmem_limit_bytes=12 * 1024 * 1024),
        name="pack",
    )(owner_map, *rows, raw, peer_raw)

    metric, own = lax.optimization_barrier((metric, own))
    factor = pl.pallas_call(
        factor_kernel,
        out_shape=jax.ShapeDtypeStruct((devices * GROUP, devices * GROUP), jnp.bfloat16),
        in_specs=[VMEM],
        out_specs=VMEM,
        compiler_params=pltpu.CompilerParams(vmem_limit_bytes=12 * 1024 * 1024),
        name="factor",
    )(metric)

    *arrived, factor = lax.optimization_barrier([hop(x, k) for k, x in enumerate(outgoing)] + [factor])
    crossed = [swap(x) for x in arrived[1:]]

    return pl.pallas_call(
        functools.partial(exchange_kernel, chips),
        out_shape=jax.ShapeDtypeStruct((2, slots * width, slots * width), jnp.float32),
        in_specs=[VMEM] * (2 * half + 2),
        out_specs=pl.BlockSpec(memory_space=pl.ANY),
        scratch_shapes=[
            pltpu.VMEM((devices * orbitals, slots * width), raw.dtype),
            pltpu.VMEM((2, slots * width, slots * width), jnp.float32),
            pltpu.SemaphoreType.DMA((2, slots)),
        ],
        compiler_params=pltpu.CompilerParams(vmem_limit_bytes=32 * 1024 * 1024),
        name="exchange",
    )(info, factor, own, arrived[0], *arrived[1:], *crossed)


def solution(mesh):
    in_specs = (
        P(("grp", "aux"), None, None, None, None),
        P("grp", None),
        P("grp"),
        P(("grp", "aux")),
    )
    out_specs = P(("grp", "aux"), None, None)
    body = functools.partial(shards, mesh.shape["aux"])
    return jax.shard_map(body, mesh=mesh, in_specs=in_specs, out_specs=out_specs, check_vma=False)
```

```python
import functools

import jax
import jax.numpy as jnp
from jax import lax
from jax.experimental import pallas as pl
from jax.experimental.pallas import tpu as pltpu
from jax.sharding import PartitionSpec as P

VMEM = pl.BlockSpec(memory_space=pltpu.VMEM)
HBM = pl.BlockSpec(memory_space=pltpu.HBM)
GROUP = 16
EARLY = 2
LIMIT = pltpu.CompilerParams(vmem_limit_bytes=12 * 1024 * 1024)


def position():
    me = lax.axis_index("aux")
    return me // 2, lax.bitwise_and(me, 1)


def factor_kernel(metric_ref, _, factor_ref):
    wide, aux = factor_ref.shape[0], metric_ref.shape[0]
    chip, core = position()
    row = lax.broadcasted_iota(jnp.int32, (wide, aux), 0) // GROUP
    column = lax.broadcasted_iota(jnp.int32, (wide, aux), 1)
    pick = (row == column).astype(jnp.bfloat16)
    place = row // 2
    far = jnp.where(place < 2, 0, lax.bitwise_and(place, 1))
    away = jnp.where(place < 2, place, lax.bitwise_xor(place, core))
    origin = 2 * lax.bitwise_xor(away, chip) + lax.bitwise_xor(lax.bitwise_xor(lax.bitwise_and(row, 1), far), core)
    pick_origin = (origin == column).astype(jnp.bfloat16)
    tall = jnp.dot(pick, metric_ref[...], preferred_element_type=jnp.float32).astype(jnp.bfloat16)
    spread = lax.dot_general(tall, pick_origin, (((1,), (1,)), ((), ())), preferred_element_type=jnp.float32)
    same = lax.rem(lax.broadcasted_iota(jnp.int32, (wide, wide), 0), GROUP) == lax.rem(
        lax.broadcasted_iota(jnp.int32, (wide, wide), 1), GROUP
    )
    factor_ref[...] = jnp.where(same, spread, 0.0).astype(jnp.bfloat16)


def place_blocks(small_ref, ids, held, sem):
    copy = pltpu.make_async_copy(small_ref, ids, sem)
    copy.start()
    copy.wait()

    def place(o, carry):
        held[ids[o]] = o
        return carry

    lax.fori_loop(0, held.shape[0], place, 0, unroll=True)


def served(k, f, chip, core):
    there = lax.bitwise_xor(chip, 2 * k + core)
    return 2 * there + (core if f == 0 else 1 - core)


def early_kernel(hops, small_ref, raw_ref, *refs):
    *outs, ids, held, sem = refs
    place_blocks(small_ref, ids, held, sem)
    blocks, tile = raw_ref.shape[0], raw_ref.shape[2]
    chip, core = position()
    lane = lax.broadcasted_iota(jnp.int32, (tile, 128), 1)
    mine = jnp.zeros((tile, 128), jnp.int32)
    for n in range(4):
        mine = jnp.where(lane == n, ids[blocks + n], mine)
    mine = mine.astype(jnp.float32).astype(jnp.bfloat16)
    for k, out in zip(hops, outs):
        if k > 0:
            for f in range(2):
                for w in range(2):
                    block = held[2 * served(k, f, chip, core) + w]
                    for s in range(EARLY):
                        out[(f * 2 + w) * EARLY + s] = raw_ref[block, s]
        if out.shape[0] % 2:
            out[out.shape[0] - 1] = mine


def counts_kernel(*refs):
    *got, out = refs
    for n, ref in enumerate(got):
        out[n : n + 1, :] = ref[ref.shape[0] - 1, 0:16, :].astype(jnp.float32)[0:1, :].astype(jnp.int32)


def late_kernel(hops, small_ref, counts_ref, crossed_ref, own_raw, peer_raw, *refs):
    outs = refs[: len(hops)]
    ids, held, direct, crossed, sem, sems = refs[-6:]
    blocks, slots = own_raw.shape[0], own_raw.shape[1]
    chip, core = position()
    copies = [
        pltpu.make_async_copy(counts_ref, direct, sems.at[0]),
        pltpu.make_async_copy(crossed_ref, crossed, sems.at[1]),
    ]
    for copy in copies:
        copy.start()
    place_blocks(small_ref, ids, held, sem)
    for copy in copies:
        copy.wait()

    def live(block):
        m = lax.bitwise_xor(block // 4, chip)
        far = lax.bitwise_and(lax.bitwise_xor(m, core), 1)
        sender = jnp.where(m >= 2, lax.bitwise_xor(core, far), core)
        line = 2 * lax.bitwise_xor(lax.bitwise_and(block // 2, 1), sender) + lax.bitwise_and(block, 1)
        near = jnp.where(m == 0, ids[blocks + line], direct[0, line])
        return jnp.where(m < 2, near, jnp.where(far == 0, direct[m // 2, line], crossed[m // 2, line]))

    def fill(target, at, raw, first, second, count, start):
        for j in range(slots - start if start == 0 else slots - 1 - start):
            from_first = j + start < count
            block = jnp.where(from_first, first, second)
            slot = jnp.where(from_first, j + start, (slots - 1 if start == 0 else slots - 2) - j)
            target[at + j] = raw[block, slot]

    def send(dest, target, start):
        first, second = held[2 * dest], held[2 * dest + 1]
        count = live(first)
        fill(target, 0, own_raw, first, second, count, start)
        fill(target, target.shape[0] // 2, peer_raw, first, second, count, start)
        return count, second

    for k, out in zip(hops, outs):
        if k > 0:
            for f in range(2):
                send(served(k, f, chip, core), out.at[f], EARLY)
        else:
            self_ref, info_ref = refs[len(hops) : len(hops) + 2]
            send(2 * lax.bitwise_xor(chip, 1) + core, out, 0)
            count, second = send(2 * chip + core, self_ref, 0)
            row = lax.broadcasted_iota(jnp.int32, info_ref.shape, 0)
            info_ref[...] = jnp.where(row == 0, count, live(second))


def forward_kernel(*refs):
    *got, out = refs
    for n, ref in enumerate(got):
        out[n * 2 * EARLY : (n + 1) * 2 * EARLY] = ref[2 * EARLY : 4 * EARLY]


def exchange_kernel(chips, info_ref, factor_ref, self_ref, side_ref, *refs):
    half = chips // 2
    first, refs = refs[: half - 1], refs[half - 1 :]
    second, refs = refs[: half - 1], refs[half - 1 :]
    forwarded, refs = refs[0], refs[1:]
    third, third_crossed, refs = refs[: half - 1], refs[half - 1 : 2 * half - 2], refs[2 * half - 2 :]
    out_ref, rows, stage, sems = refs
    doubled, orbitals, width = self_ref.shape
    slots = doubled // 2
    wide = factor_ref.shape[0]
    first_live = info_ref[0:1, :]

    def choose(s, early, late, at):
        mirror = slots - 1 - s
        ours = early(s) if s < EARLY else late(s - EARLY) if s < slots - 1 else None
        theirs = early(EARLY + mirror) if mirror < EARLY else late(slots - 2 - mirror) if mirror < slots - 1 else None
        if ours is None or theirs is None:
            return theirs if ours is None else ours
        return jnp.where(first_live > s, ours.astype(jnp.float32), theirs.astype(jnp.float32)).astype(ours.dtype)

    def pieces(s, start):
        at = slice(start, start + GROUP)
        found = []
        for ref in (self_ref, side_ref):
            found += [ref[q * slots + s, at, :] for q in range(2)]
        own_late = slots - 1 - EARLY
        for k in range(1, half):
            for f in range(2):
                late_ref = (third, third_crossed)[f][k - 1]
                for q in range(2):
                    base = q * own_late
                    if f == 0:
                        early_ref, early_base = (first, second)[q][k - 1], 0
                    else:
                        early_ref, early_base = forwarded, 2 * EARLY * (k - 1 + q * (half - 1))
                    found.append(
                        choose(
                            s,
                            lambda n, ref=early_ref, base=early_base: ref[base + n, at, :],
                            lambda n, ref=late_ref, base=base, f=f: ref[f, base + n, at, :],
                            at,
                        )
                    )
        return jnp.concatenate(found, axis=0)

    def span(n):
        return slice(n * width, (n + 1) * width)

    for part in range(orbitals // GROUP):
        columns = [pieces(s, part * GROUP) for s in range(slots)]
        fitted = jnp.dot(factor_ref[...], jnp.concatenate(columns, axis=1), preferred_element_type=jnp.float32)
        rows[part * wide : (part + 1) * wide, :] = fitted.astype(jnp.bfloat16)

    live = [info_ref[0:1, :], info_ref[1:2, :]]
    for s in range(slots):
        product = lax.dot_general(
            rows[:, span(s)], rows[...], (((0,), (0,)), ((), ())), preferred_element_type=jnp.float32
        )
        for which in range(2):
            row = s if which == 0 else slots - 1 - s
            for t in range(slots):
                column = t if which == 0 else slots - 1 - t
                stage[which, span(row), span(column)] = jnp.where(
                    live[which] > max(row, column), product[:, span(t)], 0.0
                )
            pltpu.make_async_copy(
                stage.at[which, span(row)], out_ref.at[which, span(row)], sems.at[which, row]
            ).start()
    for which in range(2):
        for row in range(slots):
            pltpu.make_async_copy(
                stage.at[which, span(row)], out_ref.at[which, span(row)], sems.at[which, row]
            ).wait()


def shards(devices, raw_tiles, metric, owner_map, counts):
    chips = devices // 2
    half = chips // 2
    _, blocks, orbitals, slots, width = raw_tiles.shape
    lines = -(-(blocks + 4) // 128) * 128
    raw = raw_tiles[0].transpose(0, 2, 1, 3)
    tie = lax.optimization_barrier

    def swap(x):
        return lax.ppermute(x, "aux", [(i, i ^ 1) for i in range(devices)])

    def hop(x, k):
        def target(i):
            away = 1 if k == 0 else 2 * k + i % 2
            return (i // 2 ^ away) * 2 + i % 2

        return lax.ppermute(x, "aux", [(i, target(i)) for i in range(devices)])

    def shape(*dims):
        return jax.ShapeDtypeStruct(dims, raw.dtype)

    factor = pl.pallas_call(
        factor_kernel,
        out_shape=shape(devices * GROUP, devices * GROUP),
        in_specs=[VMEM, HBM],
        out_specs=VMEM,
        compiler_params=pltpu.CompilerParams(vmem_limit_bytes=61 * 1024 * 1024),
        name="factor",
    )(metric, raw)
    other, factor = tie((swap(counts), factor))
    small = jnp.concatenate([owner_map, counts, other, jnp.zeros((lines - blocks - 4,), jnp.int32)])
    raw_there, small = tie((raw, small))
    peer_raw = swap(raw_there)

    far = [*reversed(range(2, half))]
    near = [1, 0]
    place = [pltpu.SMEM((lines,), jnp.int32), pltpu.SMEM((blocks,), jnp.int32)]
    one = pltpu.SemaphoreType.DMA(())

    def early(hops, raw, counted):
        return pl.pallas_call(
            functools.partial(early_kernel, hops),
            out_shape=[shape((4 * EARLY if k else 0) + counted, orbitals, width) for k in hops],
            in_specs=[VMEM] * 2,
            out_specs=[VMEM] * len(hops),
            scratch_shapes=place + [one],
            compiler_params=LIMIT,
            name="early",
        )(small, raw)

    def hops(ks, xs):
        return [hop(x, k) for k, x in zip(ks, xs)]

    first = hops(far + near, early(far + near, raw, 1))
    *second, second_near = early(far + near[:1], peer_raw, 0)
    second = hops(far, second)
    first = tie(first)[::-1]
    brought = pl.pallas_call(
        counts_kernel,
        out_shape=jax.ShapeDtypeStruct((half, 128), jnp.int32),
        in_specs=[VMEM] * half,
        out_specs=VMEM,
        compiler_params=LIMIT,
        name="counts",
    )(*first)
    brought_there = swap(brought)

    def late(ks, small, extra=()):
        own = slots - 1 - EARLY
        out_shape = [shape(2, 2 * own, orbitals, width) if k else shape(2 * slots, orbitals, width) for k in ks]
        out_shape += extra
        return pl.pallas_call(
            functools.partial(late_kernel, ks),
            out_shape=out_shape,
            in_specs=[VMEM] * 5,
            out_specs=[VMEM] * len(out_shape),
            scratch_shapes=place
            + [pltpu.SMEM((half, 128), jnp.int32)] * 2
            + [one, pltpu.SemaphoreType.DMA((2,))],
            compiler_params=LIMIT,
            cost_estimate=pl.CostEstimate(flops=0, bytes_accessed=1024, transcendentals=0),
            name="late",
        )(small, brought, brought_there, raw, peer_raw)

    *third, own, info = late(
        far + near, small, [shape(2 * slots, orbitals, width), jax.ShapeDtypeStruct((8, 128), jnp.int32)]
    )
    third, second, second_near = tie((third, second, second_near))
    second_near, *third = tie(hops(near[:1] + far + near, [second_near, *third]))
    third = third[::-1]
    second = [second_near, *second[::-1]]
    forwarded = pl.pallas_call(
        forward_kernel,
        out_shape=shape((2 * half - 2) * 2 * EARLY, orbitals, width),
        in_specs=[VMEM] * (2 * half - 2),
        out_specs=VMEM,
        compiler_params=LIMIT,
        name="forward",
    )(*first[1:], *second)
    forwarded = swap(forwarded)
    crossed = [swap(x) for x in third[1:]]

    return pl.pallas_call(
        functools.partial(exchange_kernel, chips),
        out_shape=jax.ShapeDtypeStruct((2, slots * width, slots * width), jnp.float32),
        in_specs=[VMEM] * (4 * half + 1),
        out_specs=pl.BlockSpec(memory_space=pl.ANY),
        scratch_shapes=[
            pltpu.VMEM((devices * orbitals, slots * width), raw.dtype),
            pltpu.VMEM((2, slots * width, slots * width), jnp.float32),
            pltpu.SemaphoreType.DMA((2, slots)),
        ],
        compiler_params=pltpu.CompilerParams(vmem_limit_bytes=32 * 1024 * 1024),
        name="exchange",
    )(info, factor, own, third[0], *first[1:], *second, forwarded, *third[1:], *crossed)


def solution(mesh):
    in_specs = (
        P(("grp", "aux"), None, None, None, None),
        P("grp", None),
        P("grp"),
        P(("grp", "aux")),
    )
    out_specs = P(("grp", "aux"), None, None)
    body = functools.partial(shards, mesh.shape["aux"])
    return jax.shard_map(body, mesh=mesh, in_specs=in_specs, out_specs=out_specs, check_vma=False)
```

```python
import functools

import jax
import jax.numpy as jnp
from jax import lax
from jax.experimental import pallas as pl
from jax.experimental.pallas import tpu as pltpu
from jax.sharding import PartitionSpec as P

VMEM = pl.BlockSpec(memory_space=pltpu.VMEM)
HBM = pl.BlockSpec(memory_space=pltpu.HBM)
GROUP = 16
EARLY = 2
LIMIT = pltpu.CompilerParams(vmem_limit_bytes=12 * 1024 * 1024)


def position():
    me = lax.axis_index("aux")
    return me // 2, lax.bitwise_and(me, 1)


def begin_kernel(_, out_ref):
    out_ref[...] = jnp.zeros_like(out_ref)


def factor_kernel(metric_ref, _, factor_ref):
    wide, aux = factor_ref.shape[0], metric_ref.shape[0]
    chip, core = position()
    row = lax.broadcasted_iota(jnp.int32, (wide, aux), 0) // GROUP
    column = lax.broadcasted_iota(jnp.int32, (wide, aux), 1)
    pick = (row == column).astype(jnp.bfloat16)
    place = row // 2
    far = jnp.where(place < 2, 0, lax.bitwise_and(place, 1))
    away = jnp.where(place < 2, place, lax.bitwise_xor(place, core))
    origin = 2 * lax.bitwise_xor(away, chip) + lax.bitwise_xor(lax.bitwise_xor(lax.bitwise_and(row, 1), far), core)
    pick_origin = (origin == column).astype(jnp.bfloat16)
    tall = jnp.dot(pick, metric_ref[...], preferred_element_type=jnp.float32).astype(jnp.bfloat16)
    spread = lax.dot_general(tall, pick_origin, (((1,), (1,)), ((), ())), preferred_element_type=jnp.float32)
    same = lax.rem(lax.broadcasted_iota(jnp.int32, (wide, wide), 0), GROUP) == lax.rem(
        lax.broadcasted_iota(jnp.int32, (wide, wide), 1), GROUP
    )
    factor_ref[...] = jnp.where(same, spread, 0.0).astype(jnp.bfloat16)


def place_blocks(small_ref, ids, held, sem):
    copy = pltpu.make_async_copy(small_ref, ids, sem)
    copy.start()
    copy.wait()

    def place(o, carry):
        held[ids[o]] = o
        return carry

    lax.fori_loop(0, held.shape[0], place, 0, unroll=True)


def served(k, f, chip, core):
    there = lax.bitwise_xor(chip, 2 * k + core)
    return 2 * there + (core if f == 0 else 1 - core)


def early_kernel(hops, small_ref, raw_ref, *refs):
    *outs, ids, held, sem = refs
    place_blocks(small_ref, ids, held, sem)
    blocks, tile = raw_ref.shape[0], raw_ref.shape[2]
    chip, core = position()
    lane = lax.broadcasted_iota(jnp.int32, (tile, 128), 1)
    mine = jnp.zeros((tile, 128), jnp.int32)
    for n in range(4):
        mine = jnp.where(lane == n, ids[blocks + n], mine)
    mine = mine.astype(jnp.float32).astype(jnp.bfloat16)
    for k, out in zip(hops, outs):
        if k > 0:
            for f in range(2):
                for w in range(2):
                    block = held[2 * served(k, f, chip, core) + w]
                    for s in range(EARLY):
                        out[(f * 2 + w) * EARLY + s] = raw_ref[block, s]
        if out.shape[0] % 2:
            out[out.shape[0] - 1] = mine


def counts_kernel(*refs):
    *got, out = refs
    for n, ref in enumerate(got):
        out[n : n + 1, :] = ref[ref.shape[0] - 1, 0:16, :].astype(jnp.float32)[0:1, :].astype(jnp.int32)


def late_kernel(hops, small_ref, counts_ref, crossed_ref, own_raw, peer_raw, *refs):
    outs = refs[: len(hops)]
    ids, held, direct, crossed, sem, sems = refs[-6:]
    blocks, slots = own_raw.shape[0], own_raw.shape[1]
    chip, core = position()
    copies = [
        pltpu.make_async_copy(counts_ref, direct, sems.at[0]),
        pltpu.make_async_copy(crossed_ref, crossed, sems.at[1]),
    ]
    for copy in copies:
        copy.start()
    place_blocks(small_ref, ids, held, sem)
    for copy in copies:
        copy.wait()

    def live(block):
        m = lax.bitwise_xor(block // 4, chip)
        far = lax.bitwise_and(lax.bitwise_xor(m, core), 1)
        sender = jnp.where(m >= 2, lax.bitwise_xor(core, far), core)
        line = 2 * lax.bitwise_xor(lax.bitwise_and(block // 2, 1), sender) + lax.bitwise_and(block, 1)
        near = jnp.where(m == 0, ids[blocks + line], direct[0, line])
        return jnp.where(m < 2, near, jnp.where(far == 0, direct[m // 2, line], crossed[m // 2, line]))

    def fill(target, at, raw, first, second, count, start):
        for j in range(slots - start if start == 0 else slots - 1 - start):
            from_first = j + start < count
            block = jnp.where(from_first, first, second)
            slot = jnp.where(from_first, j + start, (slots - 1 if start == 0 else slots - 2) - j)
            target[at + j] = raw[block, slot]

    def send(dest, target, start):
        first, second = held[2 * dest], held[2 * dest + 1]
        count = live(first)
        fill(target, 0, own_raw, first, second, count, start)
        fill(target, target.shape[0] // 2, peer_raw, first, second, count, start)
        return count, second

    for k, out in zip(hops, outs):
        if k > 0:
            for f in range(2):
                send(served(k, f, chip, core), out.at[f], EARLY)
        else:
            self_ref, info_ref = refs[len(hops) : len(hops) + 2]
            send(2 * lax.bitwise_xor(chip, 1) + core, out, 0)
            count, second = send(2 * chip + core, self_ref, 0)
            row = lax.broadcasted_iota(jnp.int32, info_ref.shape, 0)
            info_ref[...] = jnp.where(row == 0, count, live(second))


def forward_kernel(*refs):
    *got, out = refs
    for n, ref in enumerate(got):
        out[n * 2 * EARLY : (n + 1) * 2 * EARLY] = ref[2 * EARLY : 4 * EARLY]


def exchange_kernel(chips, info_ref, factor_ref, self_ref, side_ref, *refs):
    half = chips // 2
    first, refs = refs[: half - 1], refs[half - 1 :]
    second, refs = refs[: half - 1], refs[half - 1 :]
    forwarded, refs = refs[0], refs[1:]
    third, third_crossed, refs = refs[: half - 1], refs[half - 1 : 2 * half - 2], refs[2 * half - 2 :]
    out_ref, rows, stage, sems = refs
    doubled, orbitals, width = self_ref.shape
    slots = doubled // 2
    wide = factor_ref.shape[0]
    first_live = info_ref[0:1, :]

    def choose(s, early, late, at):
        mirror = slots - 1 - s
        ours = early(s) if s < EARLY else late(s - EARLY) if s < slots - 1 else None
        theirs = early(EARLY + mirror) if mirror < EARLY else late(slots - 2 - mirror) if mirror < slots - 1 else None
        if ours is None or theirs is None:
            return theirs if ours is None else ours
        return jnp.where(first_live > s, ours.astype(jnp.float32), theirs.astype(jnp.float32)).astype(ours.dtype)

    def pieces(s, start):
        at = slice(start, start + GROUP)
        found = []
        for ref in (self_ref, side_ref):
            found += [ref[q * slots + s, at, :] for q in range(2)]
        own_late = slots - 1 - EARLY
        for k in range(1, half):
            for f in range(2):
                late_ref = (third, third_crossed)[f][k - 1]
                for q in range(2):
                    base = q * own_late
                    if f == 0:
                        early_ref, early_base = (first, second)[q][k - 1], 0
                    else:
                        early_ref, early_base = forwarded, 2 * EARLY * (k - 1 + q * (half - 1))
                    found.append(
                        choose(
                            s,
                            lambda n, ref=early_ref, base=early_base: ref[base + n, at, :],
                            lambda n, ref=late_ref, base=base, f=f: ref[f, base + n, at, :],
                            at,
                        )
                    )
        return jnp.concatenate(found, axis=0)

    def span(n):
        return slice(n * width, (n + 1) * width)

    for part in range(orbitals // GROUP):
        columns = [pieces(s, part * GROUP) for s in range(slots)]
        fitted = jnp.dot(factor_ref[...], jnp.concatenate(columns, axis=1), preferred_element_type=jnp.float32)
        rows[part * wide : (part + 1) * wide, :] = fitted.astype(jnp.bfloat16)

    live = [info_ref[0:1, :], info_ref[1:2, :]]
    for s in range(slots):
        product = lax.dot_general(
            rows[:, span(s)], rows[...], (((0,), (0,)), ((), ())), preferred_element_type=jnp.float32
        )
        for which in range(2):
            row = s if which == 0 else slots - 1 - s
            for t in range(slots):
                column = t if which == 0 else slots - 1 - t
                stage[which, span(row), span(column)] = jnp.where(
                    live[which] > max(row, column), product[:, span(t)], 0.0
                )
            pltpu.make_async_copy(
                stage.at[which, span(row)], out_ref.at[which, span(row)], sems.at[which, row]
            ).start()
    for which in range(2):
        for row in range(slots):
            pltpu.make_async_copy(
                stage.at[which, span(row)], out_ref.at[which, span(row)], sems.at[which, row]
            ).wait()


def shards(devices, raw_tiles, metric, owner_map, counts):
    chips = devices // 2
    half = chips // 2
    _, blocks, orbitals, slots, width = raw_tiles.shape
    lines = -(-(blocks + 4) // 128) * 128
    raw = raw_tiles[0].transpose(0, 2, 1, 3)
    tie = lax.optimization_barrier

    def swap(x):
        return lax.ppermute(x, "aux", [(i, i ^ 1) for i in range(devices)])

    def hop(x, k):
        def target(i):
            away = 1 if k == 0 else 2 * k + i % 2
            return (i // 2 ^ away) * 2 + i % 2

        return lax.ppermute(x, "aux", [(i, target(i)) for i in range(devices)])

    def shape(*dims):
        return jax.ShapeDtypeStruct(dims, raw.dtype)

    began = pl.pallas_call(
        begin_kernel,
        out_shape=jax.ShapeDtypeStruct((lines,), jnp.int32),
        in_specs=[HBM],
        out_specs=VMEM,
        compiler_params=pltpu.CompilerParams(vmem_limit_bytes=61 * 1024 * 1024),
        name="begin",
    )(raw)
    other, began = tie((swap(counts), began))
    small = jnp.concatenate([owner_map, counts, other, jnp.zeros((lines - blocks - 4,), jnp.int32)])
    raw_there, small = tie((raw, small))
    peer_raw = swap(raw_there)

    far = [*reversed(range(2, half))]
    near = [1, 0]
    place = [pltpu.SMEM((lines,), jnp.int32), pltpu.SMEM((blocks,), jnp.int32)]
    one = pltpu.SemaphoreType.DMA(())

    def early(hops, raw, counted):
        return pl.pallas_call(
            functools.partial(early_kernel, hops),
            out_shape=[shape((4 * EARLY if k else 0) + counted, orbitals, width) for k in hops],
            in_specs=[VMEM] * 2,
            out_specs=[VMEM] * len(hops),
            scratch_shapes=place + [one],
            compiler_params=LIMIT,
            name="early",
        )(small, raw)

    def hops(ks, xs):
        return [hop(x, k) for k, x in zip(ks, xs)]

    first = hops(far + near, early(far + near, raw, 1))
    second = hops(far + near[:1], early(far + near[:1], peer_raw, 0))
    first = tie(first)[::-1]
    brought = pl.pallas_call(
        counts_kernel,
        out_shape=jax.ShapeDtypeStruct((half, 128), jnp.int32),
        in_specs=[VMEM] * half,
        out_specs=VMEM,
        compiler_params=LIMIT,
        name="counts",
    )(*first)
    brought_there = swap(brought)

    def late(ks, small, extra=()):
        own = slots - 1 - EARLY
        out_shape = [shape(2, 2 * own, orbitals, width) if k else shape(2 * slots, orbitals, width) for k in ks]
        out_shape += extra
        return pl.pallas_call(
            functools.partial(late_kernel, ks),
            out_shape=out_shape,
            in_specs=[VMEM] * 5,
            out_specs=[VMEM] * len(out_shape),
            scratch_shapes=place
            + [pltpu.SMEM((half, 128), jnp.int32)] * 2
            + [one, pltpu.SemaphoreType.DMA((2,))],
            compiler_params=LIMIT,
            cost_estimate=pl.CostEstimate(flops=0, bytes_accessed=1024, transcendentals=0),
            name="late",
        )(small, brought, brought_there, raw, peer_raw)

    *third, own, info = late(
        far + near, small, [shape(2 * slots, orbitals, width), jax.ShapeDtypeStruct((8, 128), jnp.int32)]
    )
    pairs = [tie((x, y)) for x, y in zip(third[: len(far)], second)]
    third = [x for x, _ in pairs] + third[len(pairs) :]
    second = [y for _, y in pairs] + second[len(pairs) :]
    metric, own_tiles = tie((metric, own))
    factor = pl.pallas_call(
        factor_kernel,
        out_shape=shape(devices * GROUP, devices * GROUP),
        in_specs=[VMEM, HBM],
        out_specs=VMEM,
        compiler_params=LIMIT,
        name="factor",
    )(metric, began)
    *third, factor = tie(hops(far + near, third) + [factor])
    third = third[::-1]
    second = second[::-1]
    forwarded = pl.pallas_call(
        forward_kernel,
        out_shape=shape((2 * half - 2) * 2 * EARLY, orbitals, width),
        in_specs=[VMEM] * (2 * half - 2),
        out_specs=VMEM,
        compiler_params=LIMIT,
        name="forward",
    )(*first[1:], *second)
    forwarded = swap(forwarded)
    crossed = [swap(x) for x in third[1:]]

    return pl.pallas_call(
        functools.partial(exchange_kernel, chips),
        out_shape=jax.ShapeDtypeStruct((2, slots * width, slots * width), jnp.float32),
        in_specs=[VMEM] * (4 * half + 1),
        out_specs=pl.BlockSpec(memory_space=pl.ANY),
        scratch_shapes=[
            pltpu.VMEM((devices * orbitals, slots * width), raw.dtype),
            pltpu.VMEM((2, slots * width, slots * width), jnp.float32),
            pltpu.SemaphoreType.DMA((2, slots)),
        ],
        compiler_params=pltpu.CompilerParams(vmem_limit_bytes=32 * 1024 * 1024),
        name="exchange",
    )(info, factor, own_tiles, third[0], *first[1:], *second, forwarded, *third[1:], *crossed)


def solution(mesh):
    in_specs = (
        P(("grp", "aux"), None, None, None, None),
        P("grp", None),
        P("grp"),
        P(("grp", "aux")),
    )
    out_specs = P(("grp", "aux"), None, None)
    body = functools.partial(shards, mesh.shape["aux"])
    return jax.shard_map(body, mesh=mesh, in_specs=in_specs, out_specs=out_specs, check_vma=False)
```

```python
import functools

import jax
import jax.numpy as jnp
from jax import lax
from jax.experimental import pallas as pl
from jax.experimental.pallas import tpu as pltpu
from jax.sharding import PartitionSpec as P

VMEM = pl.BlockSpec(memory_space=pltpu.VMEM)
HBM = pl.BlockSpec(memory_space=pltpu.HBM)
GROUP = 16
EARLY = 2
LIMIT = pltpu.CompilerParams(vmem_limit_bytes=12 * 1024 * 1024)


def position():
    me = lax.axis_index("aux")
    return me // 2, lax.bitwise_and(me, 1)


def factor_kernel(metric_ref, factor_ref):
    wide, aux = factor_ref.shape[0], metric_ref.shape[0]
    chip, core = position()
    row = lax.broadcasted_iota(jnp.int32, (wide, aux), 0) // GROUP
    column = lax.broadcasted_iota(jnp.int32, (wide, aux), 1)
    pick = (row == column).astype(jnp.bfloat16)
    place = row // 2
    far = jnp.where(place < 2, 0, lax.bitwise_and(place, 1))
    away = jnp.where(place < 2, place, lax.bitwise_xor(place, core))
    origin = 2 * lax.bitwise_xor(away, chip) + lax.bitwise_xor(lax.bitwise_xor(lax.bitwise_and(row, 1), far), core)
    pick_origin = (origin == column).astype(jnp.bfloat16)
    tall = jnp.dot(pick, metric_ref[...], preferred_element_type=jnp.float32).astype(jnp.bfloat16)
    spread = lax.dot_general(tall, pick_origin, (((1,), (1,)), ((), ())), preferred_element_type=jnp.float32)
    same = lax.rem(lax.broadcasted_iota(jnp.int32, (wide, wide), 0), GROUP) == lax.rem(
        lax.broadcasted_iota(jnp.int32, (wide, wide), 1), GROUP
    )
    factor_ref[...] = jnp.where(same, spread, 0.0).astype(jnp.bfloat16)


def place_blocks(small_ref, ids, held, sem):
    copy = pltpu.make_async_copy(small_ref, ids, sem)
    copy.start()
    copy.wait()

    def place(o, carry):
        held[ids[o]] = o
        return carry

    lax.fori_loop(0, held.shape[0], place, 0, unroll=True)


def served(k, f, chip, core):
    there = lax.bitwise_xor(chip, 2 * k + core)
    return 2 * there + (core if f == 0 else 1 - core)


def early_kernel(hops, small_ref, raw_ref, *refs):
    *outs, ids, held, sem = refs
    place_blocks(small_ref, ids, held, sem)
    blocks, tile = raw_ref.shape[0], raw_ref.shape[2]
    chip, core = position()
    lane = lax.broadcasted_iota(jnp.int32, (tile, 128), 1)
    mine = jnp.zeros((tile, 128), jnp.int32)
    for n in range(4):
        mine = jnp.where(lane == n, ids[blocks + n], mine)
    mine = mine.astype(jnp.float32).astype(jnp.bfloat16)
    for k, out in zip(hops, outs):
        if k > 0:
            for f in range(2):
                for w in range(2):
                    block = held[2 * served(k, f, chip, core) + w]
                    for s in range(EARLY):
                        out[(f * 2 + w) * EARLY + s] = raw_ref[block, s]
        if out.shape[0] % 2:
            out[out.shape[0] - 1] = mine


def counts_kernel(*refs):
    *got, out = refs
    for n, ref in enumerate(got):
        out[n : n + 1, :] = ref[ref.shape[0] - 1, 0:16, :].astype(jnp.float32)[0:1, :].astype(jnp.int32)


def late_kernel(hops, small_ref, counts_ref, crossed_ref, own_raw, peer_raw, *refs):
    outs = refs[: len(hops)]
    ids, held, direct, crossed, sem, sems = refs[-6:]
    blocks, slots = own_raw.shape[0], own_raw.shape[1] + 1
    chip, core = position()
    copies = [
        pltpu.make_async_copy(counts_ref, direct, sems.at[0]),
        pltpu.make_async_copy(crossed_ref, crossed, sems.at[1]),
    ]
    for copy in copies:
        copy.start()
    place_blocks(small_ref, ids, held, sem)
    for copy in copies:
        copy.wait()

    def live(block):
        m = lax.bitwise_xor(block // 4, chip)
        far = lax.bitwise_and(lax.bitwise_xor(m, core), 1)
        sender = jnp.where(m >= 2, lax.bitwise_xor(core, far), core)
        line = 2 * lax.bitwise_xor(lax.bitwise_and(block // 2, 1), sender) + lax.bitwise_and(block, 1)
        near = jnp.where(m == 0, ids[blocks + line], direct[0, line])
        return jnp.where(m < 2, near, jnp.where(far == 0, direct[m // 2, line], crossed[m // 2, line]))

    def fill(target, at, raw, first, second, count, start):
        for j in range(slots - start if start == 0 else slots - 1 - start):
            from_first = j + start < count
            block = jnp.where(from_first, first, second)
            slot = jnp.where(from_first, j + start, (slots - 1 if start == 0 else slots - 2) - j)
            target[at + j] = raw[block, slot]

    def send(dest, target, start):
        first, second = held[2 * dest], held[2 * dest + 1]
        count = live(first)
        fill(target, 0, own_raw, first, second, count, start)
        fill(target, target.shape[0] // 2, peer_raw, first, second, count, start)
        return count, second

    for k, out in zip(hops, outs):
        if k > 0:
            for f in range(2):
                send(served(k, f, chip, core), out.at[f], EARLY)
        else:
            self_ref, info_ref = refs[len(hops) : len(hops) + 2]
            send(2 * lax.bitwise_xor(chip, 1) + core, out, 0)
            count, second = send(2 * chip + core, self_ref, 0)
            row = lax.broadcasted_iota(jnp.int32, info_ref.shape, 0)
            info_ref[...] = jnp.where(row == 0, count, live(second))


def forward_kernel(*refs):
    *got, out = refs
    for n, ref in enumerate(got):
        out[n * 2 * EARLY : (n + 1) * 2 * EARLY] = ref[2 * EARLY : 4 * EARLY]


def blank_kernel(out_ref, zeros, sem):
    zeros[...] = jnp.zeros_like(zeros)
    height = zeros.shape[0]
    copies = [
        pltpu.make_async_copy(zeros, out_ref.at[which, n * height : (n + 1) * height], sem.at[which, n])
        for which in range(2)
        for n in range(out_ref.shape[1] // height)
    ]
    for copy in copies:
        copy.start()
    for copy in copies:
        copy.wait()


def exchange_kernel(chips, blank_ref, info_ref, factor_ref, self_ref, side_ref, *refs):
    half = chips // 2
    first, refs = refs[: half - 1], refs[half - 1 :]
    second, refs = refs[: half - 1], refs[half - 1 :]
    forwarded, refs = refs[0], refs[1:]
    third, third_crossed, refs = refs[: half - 1], refs[half - 1 : 2 * half - 2], refs[2 * half - 2 :]
    out_ref, rows, stage, live, sem, sems = refs
    copy = pltpu.make_async_copy(info_ref, live, sem)
    copy.start()
    doubled, orbitals, width = self_ref.shape
    slots = doubled // 2
    wide = factor_ref.shape[0]
    first_live = info_ref[0:1, :]

    def choose(s, early, late, at):
        mirror = slots - 1 - s
        ours = early(s) if s < EARLY else late(s - EARLY) if s < slots - 1 else None
        theirs = early(EARLY + mirror) if mirror < EARLY else late(slots - 2 - mirror) if mirror < slots - 1 else None
        if ours is None or theirs is None:
            return theirs if ours is None else ours
        return jnp.where(first_live > s, ours.astype(jnp.float32), theirs.astype(jnp.float32)).astype(ours.dtype)

    def pieces(s, start):
        at = slice(start, start + GROUP)
        found = []
        for ref in (self_ref, side_ref):
            found += [ref[q * slots + s, at, :] for q in range(2)]
        own_late = slots - 1 - EARLY
        for k in range(1, half):
            for f in range(2):
                late_ref = (third, third_crossed)[f][k - 1]
                for q in range(2):
                    base = q * own_late
                    if f == 0:
                        early_ref, early_base = (first, second)[q][k - 1], 0
                    else:
                        early_ref, early_base = forwarded, 2 * EARLY * (k - 1 + q * (half - 1))
                    found.append(
                        choose(
                            s,
                            lambda n, ref=early_ref, base=early_base: ref[base + n, at, :],
                            lambda n, ref=late_ref, base=base, f=f: ref[f, base + n, at, :],
                            at,
                        )
                    )
        return jnp.concatenate(found, axis=0)

    def span(n):
        return slice(n * width, (n + 1) * width)

    for part in range(orbitals // GROUP):
        columns = [pieces(s, part * GROUP) for s in range(slots)]
        fitted = jnp.dot(factor_ref[...], jnp.concatenate(columns, axis=1), preferred_element_type=jnp.float32)
        rows[part * wide : (part + 1) * wide, :] = fitted.astype(jnp.bfloat16)

    def tiles(s, act):
        for which in range(2):
            row = s if which == 0 else slots - 1 - s
            for t in range(slots):
                column = t if which == 0 else slots - 1 - t
                if max(row, column) < slots - 1:

                    @pl.when(max(row, column) < live[which, 0])
                    def _(which=which, row=row, column=column, t=t):
                        act(
                            pltpu.make_async_copy(
                                stage.at[span(s), span(t)],
                                out_ref.at[which, span(row), span(column)],
                                sems.at[which, row],
                            )
                        )

    for group in (range(slots - 2), range(slots - 2, slots)):
        for s in group:
            stage[span(s), :] = lax.dot_general(
                rows[:, span(s)], rows[...], (((0,), (0,)), ((), ())), preferred_element_type=jnp.float32
            )
        if 0 in group:
            copy.wait()
        for s in group:
            tiles(s, lambda copy: copy.start())
    for s in range(slots):
        tiles(s, lambda copy: copy.wait())


def shards(devices, raw_tiles, metric, owner_map, counts):
    chips = devices // 2
    half = chips // 2
    _, blocks, orbitals, slots, width = raw_tiles.shape
    lines = -(-(blocks + 4) // 128) * 128
    raw = raw_tiles[0].transpose(0, 2, 1, 3)
    tie = lax.optimization_barrier

    def swap(x):
        return lax.ppermute(x, "aux", [(i, i ^ 1) for i in range(devices)])

    def hop(x, k):
        def target(i):
            away = 1 if k == 0 else 2 * k + i % 2
            return (i // 2 ^ away) * 2 + i % 2

        return lax.ppermute(x, "aux", [(i, target(i)) for i in range(devices)])

    def shape(*dims):
        return jax.ShapeDtypeStruct(dims, raw.dtype)

    other, raw = tie((swap(counts), raw[:, : slots - 1]))
    small = jnp.concatenate([owner_map, counts, other, jnp.zeros((lines - blocks - 4,), jnp.int32)])
    raw_there, small = tie((raw, small))
    peer_raw = swap(raw_there)

    far = [*reversed(range(2, half))]
    near = [1, 0]
    place = [pltpu.SMEM((lines,), jnp.int32), pltpu.SMEM((blocks,), jnp.int32)]
    one = pltpu.SemaphoreType.DMA(())

    def early(hops, raw, counted):
        return pl.pallas_call(
            functools.partial(early_kernel, hops),
            out_shape=[shape((4 * EARLY if k else 0) + counted, orbitals, width) for k in hops],
            in_specs=[VMEM] * 2,
            out_specs=[VMEM] * len(hops),
            scratch_shapes=place + [one],
            compiler_params=LIMIT,
            name="early",
        )(small, raw)

    def hops(ks, xs):
        return [hop(x, k) for k, x in zip(ks, xs)]

    ways = far[::-1] + near
    first = hops(ways, early(ways, raw, 1))
    *second, beside = hops(ways[:-1], early(ways[:-1], peer_raw, 0))
    second = [*second[::-1], beside]
    *first, beside, side = tie(first)
    first = [side, beside, *first]
    brought = pl.pallas_call(
        counts_kernel,
        out_shape=jax.ShapeDtypeStruct((half, 128), jnp.int32),
        in_specs=[VMEM] * half,
        out_specs=VMEM,
        compiler_params=LIMIT,
        name="counts",
    )(*first)
    brought_there = swap(brought)

    def late(ks, small, extra=()):
        own = slots - 1 - EARLY
        out_shape = [shape(2, 2 * own, orbitals, width) if k else shape(2 * slots, orbitals, width) for k in ks]
        out_shape += extra
        return pl.pallas_call(
            functools.partial(late_kernel, ks),
            out_shape=out_shape,
            in_specs=[VMEM] * 5,
            out_specs=[VMEM] * len(out_shape),
            scratch_shapes=place
            + [pltpu.SMEM((half, 128), jnp.int32)] * 2
            + [one, pltpu.SemaphoreType.DMA((2,))],
            compiler_params=LIMIT,
            cost_estimate=pl.CostEstimate(flops=0, bytes_accessed=1024, transcendentals=0),
            name="late",
        )(small, brought, brought_there, raw, peer_raw)

    *third, own, info = late(
        far + near, small, [shape(2 * slots, orbitals, width), jax.ShapeDtypeStruct((8, 128), jnp.int32)]
    )
    pairs = [tie((x, y)) for x, y in zip(third[: len(far)], second)]
    third = [x for x, _ in pairs] + third[len(pairs) :]
    second = [y for _, y in pairs] + second[len(pairs) :]
    metric, own_tiles = tie((metric, own))
    factor = pl.pallas_call(
        factor_kernel,
        out_shape=shape(devices * GROUP, devices * GROUP),
        in_specs=[VMEM],
        out_specs=VMEM,
        compiler_params=LIMIT,
        name="factor",
    )(metric)
    blank = pl.pallas_call(
        lambda _, *refs: blank_kernel(*refs),
        out_shape=jax.ShapeDtypeStruct((2, slots * width, slots * width), jnp.float32),
        in_specs=[HBM],
        out_specs=HBM,
        scratch_shapes=[pltpu.VMEM((width, slots * width), jnp.float32), pltpu.SemaphoreType.DMA((2, slots))],
        compiler_params=LIMIT,
        name="blank",
    )(factor)
    *third, factor, blank = tie(hops(far + near, third) + [factor, blank])
    third = third[::-1]
    second = second[::-1]
    forwarded = pl.pallas_call(
        forward_kernel,
        out_shape=shape((2 * half - 2) * 2 * EARLY, orbitals, width),
        in_specs=[VMEM] * (2 * half - 2),
        out_specs=VMEM,
        compiler_params=LIMIT,
        name="forward",
    )(*first[1:], *second)
    forwarded = swap(forwarded)
    crossed = [swap(x) for x in third[1:]]

    return pl.pallas_call(
        functools.partial(exchange_kernel, chips),
        out_shape=jax.ShapeDtypeStruct((2, slots * width, slots * width), jnp.float32),
        in_specs=[HBM] + [VMEM] * (4 * half + 1),
        out_specs=HBM,
        scratch_shapes=[
            pltpu.VMEM((devices * orbitals, slots * width), raw.dtype),
            pltpu.VMEM((slots * width, slots * width), jnp.float32),
            pltpu.SMEM((8, 128), jnp.int32),
            one,
            pltpu.SemaphoreType.DMA((2, slots)),
        ],
        input_output_aliases={0: 0},
        compiler_params=pltpu.CompilerParams(vmem_limit_bytes=32 * 1024 * 1024),
        name="exchange",
    )(blank, info, factor, own_tiles, third[0], *first[1:], *second, forwarded, *third[1:], *crossed)


def solution(mesh):
    in_specs = (
        P(("grp", "aux"), None, None, None, None),
        P("grp", None),
        P("grp"),
        P(("grp", "aux")),
    )
    out_specs = P(("grp", "aux"), None, None)
    body = functools.partial(shards, mesh.shape["aux"])
    return jax.shard_map(body, mesh=mesh, in_specs=in_specs, out_specs=out_specs, check_vma=False)
```

```python
import functools

import jax
import jax.numpy as jnp
from jax import lax
from jax.experimental import pallas as pl
from jax.experimental.pallas import tpu as pltpu
from jax.sharding import PartitionSpec as P

VMEM = pl.BlockSpec(memory_space=pltpu.VMEM)
HBM = pl.BlockSpec(memory_space=pltpu.HBM)
GROUP = 16
EARLY = 2
LIMIT = pltpu.CompilerParams(vmem_limit_bytes=12 * 1024 * 1024)


def position():
    me = lax.axis_index("aux")
    return me // 2, lax.bitwise_and(me, 1)


def factor_kernel(metric_ref, factor_ref):
    wide, aux = factor_ref.shape[0], metric_ref.shape[0]
    chip, core = position()
    row = lax.broadcasted_iota(jnp.int32, (wide, aux), 0) // GROUP
    column = lax.broadcasted_iota(jnp.int32, (wide, aux), 1)
    pick = (row == column).astype(jnp.bfloat16)
    place = row // 2
    far = jnp.where(place < 2, 0, lax.bitwise_and(place, 1))
    away = jnp.where(place < 2, place, lax.bitwise_xor(place, core))
    origin = 2 * lax.bitwise_xor(away, chip) + lax.bitwise_xor(lax.bitwise_xor(lax.bitwise_and(row, 1), far), core)
    pick_origin = (origin == column).astype(jnp.bfloat16)
    tall = jnp.dot(pick, metric_ref[...], preferred_element_type=jnp.float32).astype(jnp.bfloat16)
    spread = lax.dot_general(tall, pick_origin, (((1,), (1,)), ((), ())), preferred_element_type=jnp.float32)
    same = lax.rem(lax.broadcasted_iota(jnp.int32, (wide, wide), 0), GROUP) == lax.rem(
        lax.broadcasted_iota(jnp.int32, (wide, wide), 1), GROUP
    )
    factor_ref[...] = jnp.where(same, spread, 0.0).astype(jnp.bfloat16)


def place_blocks(small_ref, held):
    for o in range(held.shape[0]):
        held[small_ref[0, o]] = o


def served(k, f, chip, core):
    there = lax.bitwise_xor(chip, 2 * k + core)
    return 2 * there + (core if f == 0 else 1 - core)


def early_kernel(hops, small_ref, raw_ref, *refs):
    *outs, held, ids, sem = refs
    if outs[0].shape[0] % 2:
        place_blocks(small_ref, held)
    else:
        copy = pltpu.make_async_copy(small_ref, ids, sem)
        copy.start()
        copy.wait()
        for o in range(held.shape[0]):
            held[ids[0, o]] = o
    blocks, tile = raw_ref.shape[0], raw_ref.shape[2]
    chip, core = position()
    lane = lax.broadcasted_iota(jnp.int32, (tile, 128), 1)
    mine = jnp.zeros((tile, 128), jnp.int32)
    for n in range(4):
        mine = jnp.where(lane == n, small_ref[0:1, blocks + n : blocks + n + 1], mine)
    mine = mine.astype(jnp.float32).astype(jnp.bfloat16)
    for k, out in zip(hops, outs):
        if k > 0:
            for f in range(2):
                for w in range(2):
                    block = held[2 * served(k, f, chip, core) + w]
                    for s in range(EARLY):
                        out[(f * 2 + w) * EARLY + s] = raw_ref[block, s]
        if out.shape[0] % 2:
            out[out.shape[0] - 1] = mine


def counts_kernel(*refs):
    *got, out = refs
    for n, ref in enumerate(got):
        out[n : n + 1, :] = ref[ref.shape[0] - 1, 0:16, :].astype(jnp.float32)[0:1, :].astype(jnp.int32)


def late_kernel(hops, small_ref, counts_ref, crossed_ref, own_raw, peer_raw, *refs):
    outs = refs[: len(hops)]
    held, table = refs[-2:]
    blocks, slots = own_raw.shape[0], own_raw.shape[1] + 1
    half = counts_ref.shape[0]
    chip, core = position()
    place_blocks(small_ref, held)
    for line in range(4):
        for k in range(half):
            table[4 * k + line] = counts_ref[k, line]
            table[4 * (half + k) + line] = crossed_ref[k, line]
        table[8 * half + line] = small_ref[0, blocks + line]

    def live(block):
        m = lax.bitwise_xor(block // 4, chip)
        far = lax.bitwise_and(lax.bitwise_xor(m, core), 1)
        sender = jnp.where(m >= 2, lax.bitwise_xor(core, far), core)
        line = 2 * lax.bitwise_xor(lax.bitwise_and(block // 2, 1), sender) + lax.bitwise_and(block, 1)
        row = jnp.where(m < 2, jnp.where(m == 0, 2 * half, 0), m // 2 + half * far)
        return table[4 * row + line]

    def fill(target, at, raw, first, second, count, start):
        for j in range(slots - start if start == 0 else slots - 1 - start):
            from_first = j + start < count
            block = jnp.where(from_first, first, second)
            slot = jnp.where(from_first, j + start, (slots - 1 if start == 0 else slots - 2) - j)
            target[at + j] = raw[block, slot]

    def send(dest, target, own_start, peer_start):
        first, second = held[2 * dest], held[2 * dest + 1]
        count = live(first)
        fill(target, 0, own_raw, first, second, count, own_start)
        fill(target, slots - 1 - own_start if own_start else slots, peer_raw, first, second, count, peer_start)
        return count, second

    for k, out in zip(hops, outs):
        if k > 0:
            for f in range(2):
                send(served(k, f, chip, core), out.at[f], EARLY, EARLY if k > 1 else 0)
        else:
            self_ref, info_ref = refs[len(hops) : len(hops) + 2]
            send(2 * lax.bitwise_xor(chip, 1) + core, out, 0, 0)
            count, second = send(2 * chip + core, self_ref, 0, 0)
            row = lax.broadcasted_iota(jnp.int32, info_ref.shape, 0)
            info_ref[...] = jnp.where(row == 0, count, live(second))


def forward_kernel(*refs):
    *got, out = refs
    for n, ref in enumerate(got):
        out[n * 2 * EARLY : (n + 1) * 2 * EARLY] = ref[2 * EARLY : 4 * EARLY]


def blank_kernel(out_ref, zeros, sem):
    zeros[...] = jnp.zeros_like(zeros)
    height = zeros.shape[0]
    copies = [
        pltpu.make_async_copy(zeros, out_ref.at[which, n * height : (n + 1) * height], sem.at[which, n])
        for which in range(2)
        for n in range(out_ref.shape[1] // height)
    ]
    for copy in copies:
        copy.start()
    for copy in copies:
        copy.wait()


def exchange_kernel(chips, blank_ref, info_ref, factor_ref, self_ref, side_ref, *refs):
    half = chips // 2
    first, refs = refs[: half - 1], refs[half - 1 :]
    second, refs = (None, *refs[: half - 2]), refs[half - 2 :]
    forwarded, refs = refs[0], refs[1:]
    third, third_crossed, refs = refs[: half - 1], refs[half - 1 : 2 * half - 2], refs[2 * half - 2 :]
    out_ref, rows, stage, sems = refs
    doubled, orbitals, width = self_ref.shape
    slots = doubled // 2
    wide = factor_ref.shape[0]
    first_live = info_ref[0:1, :]

    def choose(s, early, late, at):
        mirror = slots - 1 - s
        ours = early(s) if s < EARLY else late(s - EARLY) if s < slots - 1 else None
        theirs = early(EARLY + mirror) if mirror < EARLY else late(slots - 2 - mirror) if mirror < slots - 1 else None
        if ours is None or theirs is None:
            return theirs if ours is None else ours
        return jnp.where(first_live > s, ours.astype(jnp.float32), theirs.astype(jnp.float32)).astype(ours.dtype)

    def pieces(s, start):
        at = slice(start, start + GROUP)
        found = []
        for ref in (self_ref, side_ref):
            found += [ref[q * slots + s, at, :] for q in range(2)]
        own_late = slots - 1 - EARLY
        for k in range(1, half):
            for f in range(2):
                late_ref = (third, third_crossed)[f][k - 1]
                for q in range(2):
                    base = q * own_late
                    if q == 1 and k == 1:
                        found.append(late_ref[f, base + s, at, :])
                        continue
                    if f == 0:
                        early_ref, early_base = (first, second)[q][k - 1], 0
                    else:
                        early_ref, early_base = forwarded, 2 * EARLY * (k - 1 + q * (half - 2))
                    found.append(
                        choose(
                            s,
                            lambda n, ref=early_ref, base=early_base: ref[base + n, at, :],
                            lambda n, ref=late_ref, base=base, f=f: ref[f, base + n, at, :],
                            at,
                        )
                    )
        return jnp.concatenate(found, axis=0)

    def span(n):
        return slice(n * width, (n + 1) * width)

    for part in range(orbitals // GROUP):
        columns = [pieces(s, part * GROUP) for s in range(slots)]
        fitted = jnp.dot(factor_ref[...], jnp.concatenate(columns, axis=1), preferred_element_type=jnp.float32)
        rows[part * wide : (part + 1) * wide, :] = fitted.astype(jnp.bfloat16)

    live = [info_ref[which, 0] for which in range(2)]

    def tiles(s, act):
        for which in range(2):
            row = s if which == 0 else slots - 1 - s
            for t in range(slots):
                column = t if which == 0 else slots - 1 - t
                if max(row, column) < slots - 1:

                    @pl.when(max(row, column) < live[which])
                    def _(which=which, row=row, column=column, t=t):
                        act(
                            pltpu.make_async_copy(
                                stage.at[span(s), span(t)],
                                out_ref.at[which, span(row), span(column)],
                                sems.at[which, row],
                            )
                        )

    for group in (range(slots - 2), range(slots - 2, slots)):
        for s in group:
            stage[span(s), :] = lax.dot_general(
                rows[:, span(s)], rows[...], (((0,), (0,)), ((), ())), preferred_element_type=jnp.float32
            )
        for s in group:
            tiles(s, lambda copy: copy.start())
    for s in range(slots):
        tiles(s, lambda copy: copy.wait())


def shards(devices, raw_tiles, metric, owner_map, counts):
    chips = devices // 2
    half = chips // 2
    _, blocks, orbitals, slots, width = raw_tiles.shape
    lines = -(-(blocks + 4) // 128) * 128
    raw = raw_tiles[0].transpose(0, 2, 1, 3)
    tie = lax.optimization_barrier

    def swap(x):
        return lax.ppermute(x, "aux", [(i, i ^ 1) for i in range(devices)])

    def hop(x, k):
        def target(i):
            away = 1 if k == 0 else 2 * k + i % 2
            return (i // 2 ^ away) * 2 + i % 2

        return lax.ppermute(x, "aux", [(i, target(i)) for i in range(devices)])

    def shape(*dims):
        return jax.ShapeDtypeStruct(dims, raw.dtype)

    other, raw = tie((swap(counts), raw[:, : slots - 1]))
    small = jnp.concatenate([owner_map, counts, other, jnp.zeros((lines - blocks - 4,), jnp.int32)]).reshape(1, lines)
    raw_there, small = tie((raw, small))
    peer_raw = swap(raw_there)

    far = [*reversed(range(2, half))]
    near = [1, 0]
    place = pltpu.SMEM((blocks,), jnp.int32)

    def early(hops, raw, counted):
        return pl.pallas_call(
            functools.partial(early_kernel, hops),
            out_shape=[shape((4 * EARLY if k else 0) + counted, orbitals, width) for k in hops],
            in_specs=[VMEM] * 2,
            out_specs=[VMEM] * len(hops),
            scratch_shapes=[place, pltpu.SMEM((1, lines), jnp.int32), pltpu.SemaphoreType.DMA(())],
            compiler_params=LIMIT,
            name="early",
        )(small, raw)

    def hops(ks, xs):
        return [hop(x, k) for k, x in zip(ks, xs)]

    ways = far[::-1] + near
    first = hops(ways, early(ways, raw, 1))
    second = hops(ways[:-2], early(ways[:-2], peer_raw, 0))[::-1]
    *first, beside, side = tie(first)
    first = [side, beside, *first]
    brought = pl.pallas_call(
        counts_kernel,
        out_shape=jax.ShapeDtypeStruct((half, 128), jnp.int32),
        in_specs=[VMEM] * half,
        out_specs=VMEM,
        compiler_params=LIMIT,
        name="counts",
    )(*first)
    brought_there = swap(brought)

    def late(ks, small, extra=()):
        own = slots - 1 - EARLY
        tiles = [own + (own if k > 1 else slots) for k in ks]
        out_shape = [shape(2, n, orbitals, width) if k else shape(2 * slots, orbitals, width) for k, n in zip(ks, tiles)]
        out_shape += extra
        return pl.pallas_call(
            functools.partial(late_kernel, ks),
            out_shape=out_shape,
            in_specs=[VMEM] * 5,
            out_specs=[VMEM] * len(out_shape),
            scratch_shapes=[place, pltpu.SMEM((8 * half + 4,), jnp.int32)],
            compiler_params=LIMIT,
            cost_estimate=pl.CostEstimate(flops=0, bytes_accessed=1024, transcendentals=0),
            name="late",
        )(small, brought, brought_there, raw, peer_raw)

    *third, own, info = late(
        far + near, small, [shape(2 * slots, orbitals, width), jax.ShapeDtypeStruct((8, 128), jnp.int32)]
    )
    pairs = [tie((x, y)) for x, y in zip(third[: len(far)], second)]
    third = [x for x, _ in pairs] + third[len(pairs) :]
    second = [y for _, y in pairs]
    metric, own_tiles = tie((metric, own))
    factor = pl.pallas_call(
        factor_kernel,
        out_shape=shape(devices * GROUP, devices * GROUP),
        in_specs=[VMEM],
        out_specs=VMEM,
        compiler_params=LIMIT,
        name="factor",
    )(metric)
    blank = pl.pallas_call(
        lambda _, *refs: blank_kernel(*refs),
        out_shape=jax.ShapeDtypeStruct((2, slots * width, slots * width), jnp.float32),
        in_specs=[HBM],
        out_specs=HBM,
        scratch_shapes=[pltpu.VMEM((width, slots * width), jnp.float32), pltpu.SemaphoreType.DMA((2, slots))],
        compiler_params=LIMIT,
        name="blank",
    )(factor)
    *third, factor, blank = tie(hops(far + near, third) + [factor, blank])
    third = third[::-1]
    second = second[::-1]
    forwarded = pl.pallas_call(
        forward_kernel,
        out_shape=shape((2 * half - 3) * 2 * EARLY, orbitals, width),
        in_specs=[VMEM] * (2 * half - 3),
        out_specs=VMEM,
        compiler_params=LIMIT,
        name="forward",
    )(*first[1:], *second)
    forwarded = swap(forwarded)
    crossed = [swap(x) for x in third[1:]]

    return pl.pallas_call(
        functools.partial(exchange_kernel, chips),
        out_shape=jax.ShapeDtypeStruct((2, slots * width, slots * width), jnp.float32),
        in_specs=[HBM] + [VMEM] * (4 * half),
        out_specs=HBM,
        scratch_shapes=[
            pltpu.VMEM((devices * orbitals, slots * width), raw.dtype),
            pltpu.VMEM((slots * width, slots * width), jnp.float32),
            pltpu.SemaphoreType.DMA((2, slots)),
        ],
        input_output_aliases={0: 0},
        compiler_params=pltpu.CompilerParams(vmem_limit_bytes=32 * 1024 * 1024),
        name="exchange",
    )(blank, info, factor, own_tiles, third[0], *first[1:], *second, forwarded, *third[1:], *crossed)


def solution(mesh):
    in_specs = (
        P(("grp", "aux"), None, None, None, None),
        P("grp", None),
        P("grp"),
        P(("grp", "aux")),
    )
    out_specs = P(("grp", "aux"), None, None)
    body = functools.partial(shards, mesh.shape["aux"])
    return jax.shard_map(body, mesh=mesh, in_specs=in_specs, out_specs=out_specs, check_vma=False)
```

```python
import functools

import jax
import jax.numpy as jnp
from jax import lax
from jax.experimental import pallas as pl
from jax.experimental.pallas import tpu as pltpu
from jax.sharding import PartitionSpec as P

VMEM = pl.BlockSpec(memory_space=pltpu.VMEM)
HBM = pl.BlockSpec(memory_space=pltpu.HBM)
GROUP = 16
EARLY = 2
LIMIT = pltpu.CompilerParams(vmem_limit_bytes=12 * 1024 * 1024)


def position():
    me = lax.axis_index("aux")
    return me // 2, lax.bitwise_and(me, 1)


def factor_kernel(metric_ref, factor_ref):
    wide, aux = factor_ref.shape[0], metric_ref.shape[0]
    chip, core = position()
    row = lax.broadcasted_iota(jnp.int32, (wide, aux), 0) // GROUP
    column = lax.broadcasted_iota(jnp.int32, (wide, aux), 1)
    pick = (row == column).astype(jnp.bfloat16)
    place = row // 2
    far = jnp.where(place < 2, 0, lax.bitwise_and(place, 1))
    away = jnp.where(place < 2, place, lax.bitwise_xor(place, core))
    origin = 2 * lax.bitwise_xor(away, chip) + lax.bitwise_xor(lax.bitwise_xor(lax.bitwise_and(row, 1), far), core)
    pick_origin = (origin == column).astype(jnp.bfloat16)
    tall = jnp.dot(pick, metric_ref[...], preferred_element_type=jnp.float32).astype(jnp.bfloat16)
    spread = lax.dot_general(tall, pick_origin, (((1,), (1,)), ((), ())), preferred_element_type=jnp.float32)
    same = lax.rem(lax.broadcasted_iota(jnp.int32, (wide, wide), 0), GROUP) == lax.rem(
        lax.broadcasted_iota(jnp.int32, (wide, wide), 1), GROUP
    )
    factor_ref[...] = jnp.where(same, spread, 0.0).astype(jnp.bfloat16)


def place_blocks(small_ref, held):
    for o in range(held.shape[0]):
        held[small_ref[0, o]] = o


def served(k, f, chip, core):
    there = lax.bitwise_xor(chip, 2 * k + core)
    return 2 * there + (core if f == 0 else 1 - core)


def early_kernel(hops, small_ref, raw_ref, *refs):
    *outs, held, ids, sem = refs
    if outs[0].shape[0] % 2:
        place_blocks(small_ref, held)
    else:
        copy = pltpu.make_async_copy(small_ref, ids, sem)
        copy.start()
        copy.wait()
        for o in range(held.shape[0]):
            held[ids[0, o]] = o
    blocks, tile = raw_ref.shape[0], raw_ref.shape[2]
    chip, core = position()
    lane = lax.broadcasted_iota(jnp.int32, (tile, 128), 1)
    mine = jnp.zeros((tile, 128), jnp.int32)
    for n in range(4):
        mine = jnp.where(lane == n, small_ref[0:1, blocks + n : blocks + n + 1], mine)
    mine = mine.astype(jnp.float32).astype(jnp.bfloat16)
    for k, out in zip(hops, outs):
        if k > 0:
            for f in range(2):
                for w in range(2):
                    block = held[2 * served(k, f, chip, core) + w]
                    for s in range(EARLY):
                        out[(f * 2 + w) * EARLY + s] = raw_ref[block, s]
        if out.shape[0] % 2:
            out[out.shape[0] - 1] = mine


def counts_kernel(*refs):
    *got, out = refs
    for n, ref in enumerate(got):
        out[n : n + 1, :] = ref[ref.shape[0] - 1, 0:16, :].astype(jnp.float32)[0:1, :].astype(jnp.int32)


def late_kernel(hops, small_ref, counts_ref, crossed_ref, own_raw, peer_raw, *refs):
    outs = refs[: len(hops)]
    held, table = refs[-2:]
    blocks, slots = own_raw.shape[0], own_raw.shape[1] + 1
    half = counts_ref.shape[0]
    chip, core = position()
    place_blocks(small_ref, held)
    for line in range(4):
        for k in range(half):
            table[4 * k + line] = counts_ref[k, line]
            table[4 * (half + k) + line] = crossed_ref[k, line]
        table[8 * half + line] = small_ref[0, blocks + line]

    def live(block):
        m = lax.bitwise_xor(block // 4, chip)
        far = lax.bitwise_and(lax.bitwise_xor(m, core), 1)
        sender = jnp.where(m >= 2, lax.bitwise_xor(core, far), core)
        line = 2 * lax.bitwise_xor(lax.bitwise_and(block // 2, 1), sender) + lax.bitwise_and(block, 1)
        row = jnp.where(m < 2, jnp.where(m == 0, 2 * half, 0), m // 2 + half * far)
        return table[4 * row + line]

    def fill(target, at, raw, first, second, count, start):
        for j in range(slots - start if start == 0 else slots - 1 - start):
            from_first = j + start < count
            block = jnp.where(from_first, first, second)
            slot = jnp.where(from_first, j + start, (slots - 1 if start == 0 else slots - 2) - j)
            target[at + j] = raw[block, slot]

    def send(dest, target, own_start, peer_start):
        first, second = held[2 * dest], held[2 * dest + 1]
        count = live(first)
        fill(target, 0, own_raw, first, second, count, own_start)
        fill(target, slots - 1 - own_start if own_start else slots, peer_raw, first, second, count, peer_start)
        return count, second

    for k, out in zip(hops, outs):
        if k > 0:
            for f in range(2):
                send(served(k, f, chip, core), out.at[f], EARLY, EARLY if k > 1 else 0)
        else:
            self_ref, info_ref = refs[len(hops) : len(hops) + 2]
            send(2 * lax.bitwise_xor(chip, 1) + core, out, 0, 0)
            count, second = send(2 * chip + core, self_ref, 0, 0)
            row = lax.broadcasted_iota(jnp.int32, info_ref.shape, 0)
            info_ref[...] = jnp.where(row == 0, count, live(second))


def forward_kernel(*refs):
    *got, out = refs
    for n, ref in enumerate(got):
        out[n * 2 * EARLY : (n + 1) * 2 * EARLY] = ref[2 * EARLY : 4 * EARLY]


def blank_kernel(out_ref, zeros, sem):
    zeros[...] = jnp.zeros_like(zeros)
    height = zeros.shape[0]
    copies = [
        pltpu.make_async_copy(zeros, out_ref.at[which, n * height : (n + 1) * height], sem.at[which, n])
        for which in range(2)
        for n in range(out_ref.shape[1] // height)
    ]
    for copy in copies:
        copy.start()
    for copy in copies:
        copy.wait()


def exchange_kernel(chips, blank_ref, info_ref, factor_ref, self_ref, side_ref, *refs):
    half = chips // 2
    first, refs = refs[: half - 1], refs[half - 1 :]
    second, refs = (None, *refs[: half - 2]), refs[half - 2 :]
    forwarded, refs = refs[0], refs[1:]
    third, third_crossed, refs = refs[: half - 1], refs[half - 1 : 2 * half - 2], refs[2 * half - 2 :]
    out_ref, rows, stage, sems = refs
    doubled, orbitals, width = self_ref.shape
    slots = doubled // 2
    wide = factor_ref.shape[0]
    first_live = info_ref[0:1, :]

    def choose(s, early, late, at):
        mirror = slots - 1 - s
        ours = early(s) if s < EARLY else late(s - EARLY) if s < slots - 1 else None
        theirs = early(EARLY + mirror) if mirror < EARLY else late(slots - 2 - mirror) if mirror < slots - 1 else None
        if ours is None or theirs is None:
            return theirs if ours is None else ours
        return jnp.where(first_live > s, ours.astype(jnp.float32), theirs.astype(jnp.float32)).astype(ours.dtype)

    def pieces(s, start):
        at = slice(start, start + GROUP)
        found = []
        for ref in (self_ref, side_ref):
            found += [ref[q * slots + s, at, :] for q in range(2)]
        own_late = slots - 1 - EARLY
        for k in range(1, half):
            for f in range(2):
                late_ref = (third, third_crossed)[f][k - 1]
                for q in range(2):
                    base = q * own_late
                    if q == 1 and k == 1:
                        found.append(late_ref[f, base + s, at, :])
                        continue
                    if f == 0:
                        early_ref, early_base = (first, second)[q][k - 1], 0
                    else:
                        early_ref, early_base = forwarded, 2 * EARLY * (k - 1 + q * (half - 2))
                    found.append(
                        choose(
                            s,
                            lambda n, ref=early_ref, base=early_base: ref[base + n, at, :],
                            lambda n, ref=late_ref, base=base, f=f: ref[f, base + n, at, :],
                            at,
                        )
                    )
        return jnp.concatenate(found, axis=0)

    def span(n):
        return slice(n * width, (n + 1) * width)

    for part in range(orbitals // GROUP):
        columns = [pieces(s, part * GROUP) for s in range(slots)]
        fitted = jnp.dot(factor_ref[...], jnp.concatenate(columns, axis=1), preferred_element_type=jnp.float32)
        rows[part * wide : (part + 1) * wide, :] = fitted.astype(jnp.bfloat16)

    live = [info_ref[which, 0] for which in range(2)]

    def tiles(s, act):
        for which in range(2):
            row = s if which == 0 else slots - 1 - s
            for t in range(slots):
                column = t if which == 0 else slots - 1 - t
                if max(row, column) < slots - 1:

                    @pl.when(max(row, column) < live[which])
                    def _(which=which, row=row, column=column, t=t):
                        act(
                            pltpu.make_async_copy(
                                stage.at[span(s), span(t)],
                                out_ref.at[which, span(row), span(column)],
                                sems.at[which, row],
                            )
                        )

    for group in (range(slots - 2), range(slots - 2, slots)):
        for s in group:
            stage[span(s), :] = lax.dot_general(
                rows[:, span(s)], rows[...], (((0,), (0,)), ((), ())), preferred_element_type=jnp.float32
            )
        for s in group:
            tiles(s, lambda copy: copy.start())
    for s in range(slots):
        tiles(s, lambda copy: copy.wait())


def shards(devices, raw_tiles, metric, owner_map, counts):
    chips = devices // 2
    half = chips // 2
    _, blocks, orbitals, slots, width = raw_tiles.shape
    lines = -(-(blocks + 4) // 128) * 128
    raw = raw_tiles[0].transpose(0, 2, 1, 3)
    tie = lax.optimization_barrier

    def swap(x):
        return lax.ppermute(x, "aux", [(i, i ^ 1) for i in range(devices)])

    def hop(x, k):
        def target(i):
            away = 1 if k == 0 else 2 * k + i % 2
            return (i // 2 ^ away) * 2 + i % 2

        return lax.ppermute(x, "aux", [(i, target(i)) for i in range(devices)])

    def shape(*dims):
        return jax.ShapeDtypeStruct(dims, raw.dtype)

    other, raw = tie((swap(counts), raw[:, : slots - 1]))
    small = jnp.concatenate([owner_map, counts, other, jnp.zeros((lines - blocks - 4,), jnp.int32)]).reshape(1, lines)
    raw_there, small = tie((raw, small))
    peer_raw = swap(raw_there)

    far = [*reversed(range(2, half))]
    near = [1, 0]
    place = pltpu.SMEM((blocks,), jnp.int32)

    def early(hops, raw, counted):
        return pl.pallas_call(
            functools.partial(early_kernel, hops),
            out_shape=[shape((4 * EARLY if k else 0) + counted, orbitals, width) for k in hops],
            in_specs=[VMEM] * 2,
            out_specs=[VMEM] * len(hops),
            scratch_shapes=[place, pltpu.SMEM((1, lines), jnp.int32), pltpu.SemaphoreType.DMA(())],
            compiler_params=LIMIT,
            name="early",
        )(small, raw)

    def hops(ks, xs):
        return [hop(x, k) for k, x in zip(ks, xs)]

    ways = far + near
    first = hops(ways, early(ways, raw, 1))
    second = hops(far, early(far, peer_raw, 0))
    *first, beside, side = tie(first)
    first = [side, beside, *first[::-1]]
    brought = pl.pallas_call(
        counts_kernel,
        out_shape=jax.ShapeDtypeStruct((half, 128), jnp.int32),
        in_specs=[VMEM] * half,
        out_specs=VMEM,
        compiler_params=LIMIT,
        name="counts",
    )(*first)
    brought_there = swap(brought)

    def late(ks, small, extra=()):
        own = slots - 1 - EARLY
        tiles = [own + (own if k > 1 else slots) for k in ks]
        out_shape = [shape(2, n, orbitals, width) if k else shape(2 * slots, orbitals, width) for k, n in zip(ks, tiles)]
        out_shape += extra
        return pl.pallas_call(
            functools.partial(late_kernel, ks),
            out_shape=out_shape,
            in_specs=[VMEM] * 5,
            out_specs=[VMEM] * len(out_shape),
            scratch_shapes=[place, pltpu.SMEM((8 * half + 4,), jnp.int32)],
            compiler_params=LIMIT,
            cost_estimate=pl.CostEstimate(flops=0, bytes_accessed=1024, transcendentals=0),
            name="late",
        )(small, brought, brought_there, raw, peer_raw)

    *third, own, info = late(
        far + near, small, [shape(2 * slots, orbitals, width), jax.ShapeDtypeStruct((8, 128), jnp.int32)]
    )
    pairs = [tie((x, y)) for x, y in zip(third[: len(far)], second[::-1])]
    third = [x for x, _ in pairs] + third[len(pairs) :]
    second = [y for _, y in pairs][::-1]
    metric, own_tiles = tie((metric, own))
    factor = pl.pallas_call(
        factor_kernel,
        out_shape=shape(devices * GROUP, devices * GROUP),
        in_specs=[VMEM],
        out_specs=VMEM,
        compiler_params=LIMIT,
        name="factor",
    )(metric)
    blank = pl.pallas_call(
        lambda _, *refs: blank_kernel(*refs),
        out_shape=jax.ShapeDtypeStruct((2, slots * width, slots * width), jnp.float32),
        in_specs=[HBM],
        out_specs=HBM,
        scratch_shapes=[pltpu.VMEM((width, slots * width), jnp.float32), pltpu.SemaphoreType.DMA((2, slots))],
        compiler_params=LIMIT,
        name="blank",
    )(factor)
    *third, factor, blank = tie(hops(far + near, third) + [factor, blank])
    third = third[::-1]
    second = second[::-1]
    forwarded = pl.pallas_call(
        forward_kernel,
        out_shape=shape((2 * half - 3) * 2 * EARLY, orbitals, width),
        in_specs=[VMEM] * (2 * half - 3),
        out_specs=VMEM,
        compiler_params=LIMIT,
        name="forward",
    )(*first[1:], *second)
    forwarded = swap(forwarded)
    crossed = [swap(x) for x in third[1:]]

    return pl.pallas_call(
        functools.partial(exchange_kernel, chips),
        out_shape=jax.ShapeDtypeStruct((2, slots * width, slots * width), jnp.float32),
        in_specs=[HBM] + [VMEM] * (4 * half),
        out_specs=HBM,
        scratch_shapes=[
            pltpu.VMEM((devices * orbitals, slots * width), raw.dtype),
            pltpu.VMEM((slots * width, slots * width), jnp.float32),
            pltpu.SemaphoreType.DMA((2, slots)),
        ],
        input_output_aliases={0: 0},
        compiler_params=pltpu.CompilerParams(vmem_limit_bytes=32 * 1024 * 1024),
        name="exchange",
    )(blank, info, factor, own_tiles, third[0], *first[1:], *second, forwarded, *third[1:], *crossed)


def solution(mesh):
    in_specs = (
        P(("grp", "aux"), None, None, None, None),
        P("grp", None),
        P("grp"),
        P(("grp", "aux")),
    )
    out_specs = P(("grp", "aux"), None, None)
    body = functools.partial(shards, mesh.shape["aux"])
    return jax.shard_map(body, mesh=mesh, in_specs=in_specs, out_specs=out_specs, check_vma=False)
```

```python
import functools

import jax
import jax.numpy as jnp
from jax import lax
from jax.experimental import pallas as pl
from jax.experimental.pallas import tpu as pltpu
from jax.sharding import PartitionSpec as P

VMEM = pl.BlockSpec(memory_space=pltpu.VMEM)
HBM = pl.BlockSpec(memory_space=pltpu.HBM)
GROUP = 16
EARLY = 2
LIMIT = pltpu.CompilerParams(vmem_limit_bytes=12 * 1024 * 1024)


def position():
    me = lax.axis_index("aux")
    return me // 2, lax.bitwise_and(me, 1)


def factor_kernel(metric_ref, factor_ref):
    wide, aux = factor_ref.shape[0], metric_ref.shape[0]
    chip, core = position()
    row = lax.broadcasted_iota(jnp.int32, (wide, aux), 0) // GROUP
    column = lax.broadcasted_iota(jnp.int32, (wide, aux), 1)
    pick = (row == column).astype(jnp.bfloat16)
    place = row // 2
    far = jnp.where(place < 2, 0, lax.bitwise_and(place, 1))
    away = jnp.where(place < 2, place, lax.bitwise_xor(place, core))
    origin = 2 * lax.bitwise_xor(away, chip) + lax.bitwise_xor(lax.bitwise_xor(lax.bitwise_and(row, 1), far), core)
    pick_origin = (origin == column).astype(jnp.bfloat16)
    tall = jnp.dot(pick, metric_ref[...], preferred_element_type=jnp.float32).astype(jnp.bfloat16)
    spread = lax.dot_general(tall, pick_origin, (((1,), (1,)), ((), ())), preferred_element_type=jnp.float32)
    same = lax.rem(lax.broadcasted_iota(jnp.int32, (wide, wide), 0), GROUP) == lax.rem(
        lax.broadcasted_iota(jnp.int32, (wide, wide), 1), GROUP
    )
    factor_ref[...] = jnp.where(same, spread, 0.0).astype(jnp.bfloat16)


def place_blocks(small_ref, held):
    for o in range(held.shape[0]):
        held[small_ref[0, o]] = o


def served(k, f, chip, core):
    there = lax.bitwise_xor(chip, 2 * k + core)
    return 2 * there + (core if f == 0 else 1 - core)


def early_kernel(hops, small_ref, raw_ref, *refs):
    *outs, held = refs
    place_blocks(small_ref, held)
    blocks, tile = raw_ref.shape[0], raw_ref.shape[2]
    chip, core = position()
    lane = lax.broadcasted_iota(jnp.int32, (tile, 128), 1)
    mine = jnp.zeros((tile, 128), jnp.int32)
    for n in range(4):
        mine = jnp.where(lane == n, small_ref[0:1, blocks + n : blocks + n + 1], mine)
    mine = mine.astype(jnp.float32).astype(jnp.bfloat16)
    for k, out in zip(hops, outs):
        if k > 0:
            for f in range(2):
                for w in range(2):
                    block = held[2 * served(k, f, chip, core) + w]
                    for s in range(EARLY):
                        out[(f * 2 + w) * EARLY + s] = raw_ref[block, s]
        if out.shape[0] % 2:
            out[out.shape[0] - 1] = mine


def counts_kernel(*refs):
    *got, out = refs
    for n, ref in enumerate(got):
        out[n : n + 1, :] = ref[ref.shape[0] - 1, 0:16, :].astype(jnp.float32)[0:1, :].astype(jnp.int32)


def late_kernel(hops, small_ref, counts_ref, crossed_ref, own_raw, peer_raw, *refs):
    outs = refs[: len(hops)]
    held, table = refs[-2:]
    blocks, slots = own_raw.shape[0], own_raw.shape[1] + 1
    half = counts_ref.shape[0]
    chip, core = position()
    place_blocks(small_ref, held)
    for line in range(4):
        for k in range(half):
            table[4 * k + line] = counts_ref[k, line]
            table[4 * (half + k) + line] = crossed_ref[k, line]
        table[8 * half + line] = small_ref[0, blocks + line]

    def live(block):
        m = lax.bitwise_xor(block // 4, chip)
        far = lax.bitwise_and(lax.bitwise_xor(m, core), 1)
        sender = jnp.where(m >= 2, lax.bitwise_xor(core, far), core)
        line = 2 * lax.bitwise_xor(lax.bitwise_and(block // 2, 1), sender) + lax.bitwise_and(block, 1)
        row = jnp.where(m < 2, jnp.where(m == 0, 2 * half, 0), m // 2 + half * far)
        return table[4 * row + line]

    def fill(target, at, raw, first, second, count, start):
        for j in range(slots - start if start == 0 else slots - 1 - start):
            from_first = j + start < count
            block = jnp.where(from_first, first, second)
            slot = jnp.where(from_first, j + start, (slots - 1 if start == 0 else slots - 2) - j)
            target[at + j] = raw[block, slot]

    def send(dest, target, own_start, peer_start):
        first, second = held[2 * dest], held[2 * dest + 1]
        count = live(first)
        fill(target, 0, own_raw, first, second, count, own_start)
        fill(target, slots - 1 - own_start if own_start else slots, peer_raw, first, second, count, peer_start)
        return count, second

    for k, out in zip(hops, outs):
        if k > 0:
            for f in range(2):
                send(served(k, f, chip, core), out.at[f], EARLY, EARLY if k > 1 else 0)
        else:
            self_ref, info_ref = refs[len(hops) : len(hops) + 2]
            send(2 * lax.bitwise_xor(chip, 1) + core, out, 0, 0)
            count, second = send(2 * chip + core, self_ref, 0, 0)
            row = lax.broadcasted_iota(jnp.int32, info_ref.shape, 0)
            info_ref[...] = jnp.where(row == 0, count, live(second))


def forward_kernel(*refs):
    *got, out = refs
    for n, ref in enumerate(got):
        out[n * 2 * EARLY : (n + 1) * 2 * EARLY] = ref[2 * EARLY : 4 * EARLY]


def blank_kernel(out_ref, zeros, sem):
    zeros[...] = jnp.zeros_like(zeros)
    height = zeros.shape[0]
    copies = [
        pltpu.make_async_copy(zeros, out_ref.at[which, n * height : (n + 1) * height], sem.at[which, n])
        for which in range(2)
        for n in range(out_ref.shape[1] // height)
    ]
    for copy in copies:
        copy.start()
    for copy in copies:
        copy.wait()


def exchange_kernel(chips, blank_ref, info_ref, factor_ref, self_ref, side_ref, *refs):
    half = chips // 2
    first, refs = refs[: half - 1], refs[half - 1 :]
    second, refs = (None, *refs[: half - 2]), refs[half - 2 :]
    forwarded, refs = refs[0], refs[1:]
    third, third_crossed, refs = refs[: half - 1], refs[half - 1 : 2 * half - 2], refs[2 * half - 2 :]
    out_ref, rows, stage, sems = refs
    doubled, orbitals, width = self_ref.shape
    slots = doubled // 2
    wide = factor_ref.shape[0]
    first_live = info_ref[0:1, :]

    def choose(s, early, late, at):
        mirror = slots - 1 - s
        ours = early(s) if s < EARLY else late(s - EARLY) if s < slots - 1 else None
        theirs = early(EARLY + mirror) if mirror < EARLY else late(slots - 2 - mirror) if mirror < slots - 1 else None
        if ours is None or theirs is None:
            return theirs if ours is None else ours
        return jnp.where(first_live > s, ours.astype(jnp.float32), theirs.astype(jnp.float32)).astype(ours.dtype)

    def pieces(s, start):
        at = slice(start, start + GROUP)
        found = []
        for ref in (self_ref, side_ref):
            found += [ref[q * slots + s, at, :] for q in range(2)]
        own_late = slots - 1 - EARLY
        for k in range(1, half):
            for f in range(2):
                late_ref = (third, third_crossed)[f][k - 1]
                for q in range(2):
                    base = q * own_late
                    if q == 1 and k == 1:
                        found.append(late_ref[f, base + s, at, :])
                        continue
                    if f == 0:
                        early_ref, early_base = (first, second)[q][k - 1], 0
                    else:
                        early_ref, early_base = forwarded, 2 * EARLY * (k - 1 + q * (half - 2))
                    found.append(
                        choose(
                            s,
                            lambda n, ref=early_ref, base=early_base: ref[base + n, at, :],
                            lambda n, ref=late_ref, base=base, f=f: ref[f, base + n, at, :],
                            at,
                        )
                    )
        return jnp.concatenate(found, axis=0)

    def span(n):
        return slice(n * width, (n + 1) * width)

    for part in range(orbitals // GROUP):
        columns = [pieces(s, part * GROUP) for s in range(slots)]
        fitted = jnp.dot(factor_ref[...], jnp.concatenate(columns, axis=1), preferred_element_type=jnp.float32)
        rows[part * wide : (part + 1) * wide, :] = fitted.astype(jnp.bfloat16)

    live = [info_ref[which, 0] for which in range(2)]

    def tiles(s, act):
        for which in range(2):
            row = s if which == 0 else slots - 1 - s
            for t in range(slots):
                column = t if which == 0 else slots - 1 - t
                if max(row, column) < slots - 1:

                    @pl.when(max(row, column) < live[which])
                    def _(which=which, row=row, column=column, t=t):
                        act(
                            pltpu.make_async_copy(
                                stage.at[span(s), span(t)],
                                out_ref.at[which, span(row), span(column)],
                                sems.at[which, row],
                            )
                        )

    for group in [range(n, n + 2) for n in range(0, slots, 2)]:
        for s in group:
            stage[span(s), :] = lax.dot_general(
                rows[:, span(s)], rows[...], (((0,), (0,)), ((), ())), preferred_element_type=jnp.float32
            )
        for s in group:
            tiles(s, lambda copy: copy.start())
    for s in range(slots):
        tiles(s, lambda copy: copy.wait())


def shards(devices, raw_tiles, metric, owner_map, counts):
    chips = devices // 2
    half = chips // 2
    _, blocks, orbitals, slots, width = raw_tiles.shape
    lines = -(-(blocks + 4) // 128) * 128
    raw = raw_tiles[0].transpose(0, 2, 1, 3)
    tie = lax.optimization_barrier

    def swap(x):
        return lax.ppermute(x, "aux", [(i, i ^ 1) for i in range(devices)])

    def hop(x, k):
        def target(i):
            away = 1 if k == 0 else 2 * k + i % 2
            return (i // 2 ^ away) * 2 + i % 2

        return lax.ppermute(x, "aux", [(i, target(i)) for i in range(devices)])

    def shape(*dims):
        return jax.ShapeDtypeStruct(dims, raw.dtype)

    other, raw = tie((swap(counts), raw[:, : slots - 1]))
    small = jnp.concatenate([owner_map, counts, other, jnp.zeros((lines - blocks - 4,), jnp.int32)]).reshape(1, lines)
    raw_there, small = tie((raw, small))
    factor = pl.pallas_call(
        factor_kernel,
        out_shape=shape(devices * GROUP, devices * GROUP),
        in_specs=[VMEM],
        out_specs=VMEM,
        compiler_params=LIMIT,
        name="factor",
    )(metric)
    peer_raw, factor = tie((swap(raw_there), factor))

    far = [*reversed(range(2, half))]
    near = [1, 0]
    place = pltpu.SMEM((blocks,), jnp.int32)

    def early(hops, raw, counted):
        return pl.pallas_call(
            functools.partial(early_kernel, hops),
            out_shape=[shape((4 * EARLY if k else 0) + counted, orbitals, width) for k in hops],
            in_specs=[VMEM] * 2,
            out_specs=[VMEM] * len(hops),
            scratch_shapes=[place],
            compiler_params=LIMIT,
            name="early",
        )(small, raw)

    def hops(ks, xs):
        return [hop(x, k) for k, x in zip(ks, xs)]

    ways = far + near
    first = hops(ways, early(ways, raw, 1))
    second = hops(far, early(far, peer_raw, 0))
    *first, beside, side = tie(first)
    first = [side, beside, *first[::-1]]
    brought = pl.pallas_call(
        counts_kernel,
        out_shape=jax.ShapeDtypeStruct((half, 128), jnp.int32),
        in_specs=[VMEM] * half,
        out_specs=VMEM,
        compiler_params=LIMIT,
        name="counts",
    )(*first)
    brought_there = swap(brought)

    def late(ks, small, extra=()):
        own = slots - 1 - EARLY
        tiles = [own + (own if k > 1 else slots) for k in ks]
        out_shape = [shape(2, n, orbitals, width) if k else shape(2 * slots, orbitals, width) for k, n in zip(ks, tiles)]
        out_shape += extra
        return pl.pallas_call(
            functools.partial(late_kernel, ks),
            out_shape=out_shape,
            in_specs=[VMEM] * 5,
            out_specs=[VMEM] * len(out_shape),
            scratch_shapes=[place, pltpu.SMEM((8 * half + 4,), jnp.int32)],
            compiler_params=LIMIT,
            cost_estimate=pl.CostEstimate(flops=0, bytes_accessed=1024, transcendentals=0),
            name="late",
        )(small, brought, brought_there, raw, peer_raw)

    *third, own, info = late(
        far + near, small, [shape(2 * slots, orbitals, width), jax.ShapeDtypeStruct((8, 128), jnp.int32)]
    )
    pairs = [tie((x, y)) for x, y in zip(third[: len(far)], second[::-1])]
    third = [x for x, _ in pairs] + third[len(pairs) :]
    second = [y for _, y in pairs][::-1]
    own_tiles = own
    blank = pl.pallas_call(
        lambda _, *refs: blank_kernel(*refs),
        out_shape=jax.ShapeDtypeStruct((2, slots * width, slots * width), jnp.float32),
        in_specs=[HBM],
        out_specs=HBM,
        scratch_shapes=[pltpu.VMEM((width, slots * width), jnp.float32), pltpu.SemaphoreType.DMA((2, slots))],
        compiler_params=LIMIT,
        name="blank",
    )(info)
    *third, blank = tie(hops(far + near, third) + [blank])
    third = third[::-1]
    second = second[::-1]
    forwarded = pl.pallas_call(
        forward_kernel,
        out_shape=shape((2 * half - 3) * 2 * EARLY, orbitals, width),
        in_specs=[VMEM] * (2 * half - 3),
        out_specs=VMEM,
        compiler_params=LIMIT,
        name="forward",
    )(*first[1:], *second)
    forwarded = swap(forwarded)
    crossed = [swap(x) for x in third[1:]]

    return pl.pallas_call(
        functools.partial(exchange_kernel, chips),
        out_shape=jax.ShapeDtypeStruct((2, slots * width, slots * width), jnp.float32),
        in_specs=[HBM] + [VMEM] * (4 * half),
        out_specs=HBM,
        scratch_shapes=[
            pltpu.VMEM((devices * orbitals, slots * width), raw.dtype),
            pltpu.VMEM((slots * width, slots * width), jnp.float32),
            pltpu.SemaphoreType.DMA((2, slots)),
        ],
        input_output_aliases={0: 0},
        compiler_params=pltpu.CompilerParams(vmem_limit_bytes=32 * 1024 * 1024),
        name="exchange",
    )(blank, info, factor, own_tiles, third[0], *first[1:], *second, forwarded, *third[1:], *crossed)


def solution(mesh):
    in_specs = (
        P(("grp", "aux"), None, None, None, None),
        P("grp", None),
        P("grp"),
        P(("grp", "aux")),
    )
    out_specs = P(("grp", "aux"), None, None)
    body = functools.partial(shards, mesh.shape["aux"])
    return jax.shard_map(body, mesh=mesh, in_specs=in_specs, out_specs=out_specs, check_vma=False)
```

```python
import functools

import jax
import jax.numpy as jnp
from jax import lax
from jax.experimental import pallas as pl
from jax.experimental.pallas import tpu as pltpu
from jax.sharding import PartitionSpec as P

VMEM = pl.BlockSpec(memory_space=pltpu.VMEM)
HBM = pl.BlockSpec(memory_space=pltpu.HBM)
GROUP = 16
EARLY = 2
LIMIT = pltpu.CompilerParams(vmem_limit_bytes=12 * 1024 * 1024)


def position():
    me = lax.axis_index("aux")
    return me // 2, lax.bitwise_and(me, 1)


def factor_kernel(metric_ref, factor_ref):
    wide, aux = factor_ref.shape[0], metric_ref.shape[0]
    chip, core = position()
    row = lax.broadcasted_iota(jnp.int32, (wide, aux), 0) // GROUP
    column = lax.broadcasted_iota(jnp.int32, (wide, aux), 1)
    pick = (row == column).astype(jnp.bfloat16)
    place = row // 2
    far = jnp.where(place < 2, 0, lax.bitwise_and(place, 1))
    away = jnp.where(place < 2, place, lax.bitwise_xor(place, core))
    origin = 2 * lax.bitwise_xor(away, chip) + lax.bitwise_xor(lax.bitwise_xor(lax.bitwise_and(row, 1), far), core)
    pick_origin = (origin == column).astype(jnp.bfloat16)
    tall = jnp.dot(pick, metric_ref[...], preferred_element_type=jnp.float32).astype(jnp.bfloat16)
    spread = lax.dot_general(tall, pick_origin, (((1,), (1,)), ((), ())), preferred_element_type=jnp.float32)
    same = lax.rem(lax.broadcasted_iota(jnp.int32, (wide, wide), 0), GROUP) == lax.rem(
        lax.broadcasted_iota(jnp.int32, (wide, wide), 1), GROUP
    )
    factor_ref[...] = jnp.where(same, spread, 0.0).astype(jnp.bfloat16)


def place_blocks(small_ref, held):
    for o in range(held.shape[0]):
        held[small_ref[0, o]] = o


def served(k, f, chip, core):
    there = lax.bitwise_xor(chip, 2 * k + core)
    return 2 * there + (core if f == 0 else 1 - core)


def early_kernel(hops, small_ref, raw_ref, *refs):
    *outs, held = refs
    place_blocks(small_ref, held)
    blocks, tile = raw_ref.shape[0], raw_ref.shape[2]
    chip, core = position()
    lane = lax.broadcasted_iota(jnp.int32, (tile, 128), 1)
    mine = jnp.zeros((tile, 128), jnp.int32)
    for n in range(4):
        mine = jnp.where(lane == n, small_ref[0:1, blocks + n : blocks + n + 1], mine)
    mine = mine.astype(jnp.float32).astype(jnp.bfloat16)
    for k, out in zip(hops, outs):
        if k > 0:
            for f in range(2):
                for w in range(2):
                    block = held[2 * served(k, f, chip, core) + w]
                    for s in range(EARLY):
                        out[(f * 2 + w) * EARLY + s] = raw_ref[block, s]
        if out.shape[0] % 2:
            out[out.shape[0] - 1] = mine


def counts_kernel(*refs):
    *got, out = refs
    for n, ref in enumerate(got):
        out[n : n + 1, :] = ref[ref.shape[0] - 1, 0:16, :].astype(jnp.float32)[0:1, :].astype(jnp.int32)


def late_kernel(hops, small_ref, counts_ref, crossed_ref, own_raw, peer_raw, *refs):
    outs = refs[: len(hops)]
    held, table = refs[-2:]
    blocks, slots = own_raw.shape[0], own_raw.shape[1] + 1
    half = counts_ref.shape[0]
    chip, core = position()
    place_blocks(small_ref, held)
    for line in range(4):
        for k in range(half):
            table[4 * k + line] = counts_ref[k, line]
            table[4 * (half + k) + line] = crossed_ref[k, line]
        table[8 * half + line] = small_ref[0, blocks + line]

    def live(block):
        m = lax.bitwise_xor(block // 4, chip)
        far = lax.bitwise_and(lax.bitwise_xor(m, core), 1)
        sender = jnp.where(m >= 2, lax.bitwise_xor(core, far), core)
        line = 2 * lax.bitwise_xor(lax.bitwise_and(block // 2, 1), sender) + lax.bitwise_and(block, 1)
        row = jnp.where(m < 2, jnp.where(m == 0, 2 * half, 0), m // 2 + half * far)
        return table[4 * row + line]

    def fill(target, at, raw, first, second, count, start):
        for j in range(slots - start if start == 0 else slots - 1 - start):
            from_first = j + start < count
            block = jnp.where(from_first, first, second)
            slot = jnp.where(from_first, j + start, (slots - 1 if start == 0 else slots - 2) - j)
            target[at + j] = raw[block, slot]

    def send(dest, target, own_start, peer_start):
        first, second = held[2 * dest], held[2 * dest + 1]
        count = live(first)
        fill(target, 0, own_raw, first, second, count, own_start)
        fill(target, slots - 1 - own_start if own_start else slots, peer_raw, first, second, count, peer_start)
        return count, second

    for k, out in zip(hops, outs):
        if k > 0:
            for f in range(2):
                send(served(k, f, chip, core), out.at[f], EARLY, EARLY if k > 1 else 0)
        else:
            self_ref, info_ref = refs[len(hops) : len(hops) + 2]
            send(2 * lax.bitwise_xor(chip, 1) + core, out, 0, 0)
            count, second = send(2 * chip + core, self_ref, 0, 0)
            row = lax.broadcasted_iota(jnp.int32, info_ref.shape, 0)
            info_ref[...] = jnp.where(row == 0, count, live(second))


def cross_kernel(*refs):
    *got, out = refs
    at = 0
    for ref in got:
        late = len(ref.shape) == 4
        tiles = ref.shape[1] if late else 2 * EARLY
        out[at : at + tiles] = ref[1] if late else ref[2 * EARLY : 4 * EARLY]
        at += tiles


def blank_kernel(out_ref, zeros, sem):
    zeros[...] = jnp.zeros_like(zeros)
    height = zeros.shape[0]
    copies = [
        pltpu.make_async_copy(zeros, out_ref.at[which, n * height : (n + 1) * height], sem.at[which, n])
        for which in range(2)
        for n in range(out_ref.shape[1] // height)
    ]
    for copy in copies:
        copy.start()
    for copy in copies:
        copy.wait()


def exchange_kernel(chips, blank_ref, info_ref, factor_ref, self_ref, side_ref, *refs):
    half = chips // 2
    first, refs = refs[: half - 1], refs[half - 1 :]
    second, refs = (None, *refs[: half - 2]), refs[half - 2 :]
    third, crossed, refs = refs[: half - 1], refs[half - 1], refs[half:]
    out_ref, rows, stage, sems = refs
    doubled, orbitals, width = self_ref.shape
    slots = doubled // 2
    wide = factor_ref.shape[0]
    first_live = info_ref[0:1, :]

    def choose(s, early, late, at):
        mirror = slots - 1 - s
        ours = early(s) if s < EARLY else late(s - EARLY) if s < slots - 1 else None
        theirs = early(EARLY + mirror) if mirror < EARLY else late(slots - 2 - mirror) if mirror < slots - 1 else None
        if ours is None or theirs is None:
            return theirs if ours is None else ours
        return jnp.where(first_live > s, ours.astype(jnp.float32), theirs.astype(jnp.float32)).astype(ours.dtype)

    def pieces(s, start):
        at = slice(start, start + GROUP)
        found = []
        for ref in (self_ref, side_ref):
            found += [ref[q * slots + s, at, :] for q in range(2)]
        own_late = slots - 1 - EARLY
        for k in range(1, half):
            for f in range(2):
                tiles = third[k - 1].shape[1]
                skip = (2 * half - 3) * 2 * EARLY + sum(ref.shape[1] for ref in third[: k - 1])
                late_ref = crossed.at[skip : skip + tiles] if f else third[k - 1].at[0]
                for q in range(2):
                    base = q * own_late
                    if q == 1 and k == 1:
                        found.append(late_ref[base + s, at, :])
                        continue
                    if f == 0:
                        early_ref, early_base = (first, second)[q][k - 1], 0
                    else:
                        early_ref, early_base = crossed, 2 * EARLY * (k - 1 + q * (half - 2))
                    found.append(
                        choose(
                            s,
                            lambda n, ref=early_ref, base=early_base: ref[base + n, at, :],
                            lambda n, ref=late_ref, base=base: ref[base + n, at, :],
                            at,
                        )
                    )
        return jnp.concatenate(found, axis=0)

    def span(n):
        return slice(n * width, (n + 1) * width)

    for part in range(orbitals // GROUP):
        columns = [pieces(s, part * GROUP) for s in range(slots)]
        fitted = jnp.dot(factor_ref[...], jnp.concatenate(columns, axis=1), preferred_element_type=jnp.float32)
        rows[part * wide : (part + 1) * wide, :] = fitted.astype(jnp.bfloat16)

    live = [info_ref[which, 0] for which in range(2)]

    def tiles(s, act):
        for which in range(2):
            row = s if which == 0 else slots - 1 - s
            for t in range(slots):
                column = t if which == 0 else slots - 1 - t
                if max(row, column) < slots - 1:

                    @pl.when(max(row, column) < live[which])
                    def _(which=which, row=row, column=column, t=t):
                        act(
                            pltpu.make_async_copy(
                                stage.at[span(s), span(t)],
                                out_ref.at[which, span(row), span(column)],
                                sems.at[which, row],
                            )
                        )

    for group in [range(n, n + 2) for n in range(0, slots, 2)]:
        for s in group:
            stage[span(s), :] = lax.dot_general(
                rows[:, span(s)], rows[...], (((0,), (0,)), ((), ())), preferred_element_type=jnp.float32
            )
        for s in group:
            tiles(s, lambda copy: copy.start())
    for s in range(slots):
        tiles(s, lambda copy: copy.wait())


def shards(devices, raw_tiles, metric, owner_map, counts):
    chips = devices // 2
    half = chips // 2
    _, blocks, orbitals, slots, width = raw_tiles.shape
    lines = -(-(blocks + 4) // 128) * 128
    raw = raw_tiles[0].transpose(0, 2, 1, 3)
    tie = lax.optimization_barrier

    def swap(x):
        return lax.ppermute(x, "aux", [(i, i ^ 1) for i in range(devices)])

    def hop(x, k):
        def target(i):
            away = 1 if k == 0 else 2 * k + i % 2
            return (i // 2 ^ away) * 2 + i % 2

        return lax.ppermute(x, "aux", [(i, target(i)) for i in range(devices)])

    def shape(*dims):
        return jax.ShapeDtypeStruct(dims, raw.dtype)

    other, raw = tie((swap(counts), raw[:, : slots - 1]))
    small = jnp.concatenate([owner_map, counts, other, jnp.zeros((lines - blocks - 4,), jnp.int32)]).reshape(1, lines)
    raw_there, small = tie((raw, small))
    factor = pl.pallas_call(
        factor_kernel,
        out_shape=shape(devices * GROUP, devices * GROUP),
        in_specs=[VMEM],
        out_specs=VMEM,
        compiler_params=LIMIT,
        name="factor",
    )(metric)
    peer_raw, factor = tie((swap(raw_there), factor))

    far = [*reversed(range(2, half))]
    near = [1, 0]
    place = pltpu.SMEM((blocks,), jnp.int32)

    def early(hops, raw, counted):
        return pl.pallas_call(
            functools.partial(early_kernel, hops),
            out_shape=[shape((4 * EARLY if k else 0) + counted, orbitals, width) for k in hops],
            in_specs=[VMEM] * 2,
            out_specs=[VMEM] * len(hops),
            scratch_shapes=[place],
            compiler_params=LIMIT,
            name="early",
        )(small, raw)

    def hops(ks, xs):
        return [hop(x, k) for k, x in zip(ks, xs)]

    ways = far + near
    first = hops(ways, early(ways, raw, 1))
    second = hops(far, early(far, peer_raw, 0))
    *first, beside, side = tie(first)
    first = [side, beside, *first[::-1]]
    brought = pl.pallas_call(
        counts_kernel,
        out_shape=jax.ShapeDtypeStruct((half, 128), jnp.int32),
        in_specs=[VMEM] * half,
        out_specs=VMEM,
        compiler_params=LIMIT,
        name="counts",
    )(*first)
    brought_there = swap(brought)

    def late(ks, small, extra=()):
        own = slots - 1 - EARLY
        tiles = [own + (own if k > 1 else slots) for k in ks]
        out_shape = [shape(2, n, orbitals, width) if k else shape(2 * slots, orbitals, width) for k, n in zip(ks, tiles)]
        out_shape += extra
        return pl.pallas_call(
            functools.partial(late_kernel, ks),
            out_shape=out_shape,
            in_specs=[VMEM] * 5,
            out_specs=[VMEM] * len(out_shape),
            scratch_shapes=[place, pltpu.SMEM((8 * half + 4,), jnp.int32)],
            compiler_params=LIMIT,
            cost_estimate=pl.CostEstimate(flops=0, bytes_accessed=1024, transcendentals=0),
            name="late",
        )(small, brought, brought_there, raw, peer_raw)

    *third, own, info = late(
        far + near, small, [shape(2 * slots, orbitals, width), jax.ShapeDtypeStruct((8, 128), jnp.int32)]
    )
    pairs = [tie((x, y)) for x, y in zip(third[: len(far)], second[::-1])]
    third = [x for x, _ in pairs] + third[len(pairs) :]
    second = [y for _, y in pairs][::-1]
    own_tiles = own
    blank = pl.pallas_call(
        lambda _, *refs: blank_kernel(*refs),
        out_shape=jax.ShapeDtypeStruct((2, slots * width, slots * width), jnp.float32),
        in_specs=[HBM],
        out_specs=HBM,
        scratch_shapes=[pltpu.VMEM((width, slots * width), jnp.float32), pltpu.SemaphoreType.DMA((2, slots))],
        compiler_params=LIMIT,
        name="blank",
    )(info)
    *third, blank = tie(hops(far + near, third) + [blank])
    third = third[::-1]
    second = second[::-1]
    crossed = pl.pallas_call(
        cross_kernel,
        out_shape=shape((2 * half - 3) * 2 * EARLY + sum(x.shape[1] for x in third[1:]), orbitals, width),
        in_specs=[VMEM] * (3 * half - 4),
        out_specs=VMEM,
        compiler_params=LIMIT,
        name="cross",
    )(*first[1:], *second, *third[1:])
    crossed = swap(crossed)

    return pl.pallas_call(
        functools.partial(exchange_kernel, chips),
        out_shape=jax.ShapeDtypeStruct((2, slots * width, slots * width), jnp.float32),
        in_specs=[HBM] + [VMEM] * (3 * half + 1),
        out_specs=HBM,
        scratch_shapes=[
            pltpu.VMEM((devices * orbitals, slots * width), raw.dtype),
            pltpu.VMEM((slots * width, slots * width), jnp.float32),
            pltpu.SemaphoreType.DMA((2, slots)),
        ],
        input_output_aliases={0: 0},
        compiler_params=pltpu.CompilerParams(vmem_limit_bytes=32 * 1024 * 1024),
        name="exchange",
    )(blank, info, factor, own_tiles, third[0], *first[1:], *second, *third[1:], crossed)


def solution(mesh):
    in_specs = (
        P(("grp", "aux"), None, None, None, None),
        P("grp", None),
        P("grp"),
        P(("grp", "aux")),
    )
    out_specs = P(("grp", "aux"), None, None)
    body = functools.partial(shards, mesh.shape["aux"])
    return jax.shard_map(body, mesh=mesh, in_specs=in_specs, out_specs=out_specs, check_vma=False)
```

```python
import functools

import jax
import jax.numpy as jnp
from jax import lax
from jax.experimental import pallas as pl
from jax.experimental.pallas import tpu as pltpu
from jax.sharding import PartitionSpec as P

VMEM = pl.BlockSpec(memory_space=pltpu.VMEM)
HBM = pl.BlockSpec(memory_space=pltpu.HBM)
GROUP = 16
EARLY = 2
LIMIT = pltpu.CompilerParams(vmem_limit_bytes=12 * 1024 * 1024)


def position():
    me = lax.axis_index("aux")
    return me // 2, lax.bitwise_and(me, 1)


def factor_kernel(metric_ref, factor_ref):
    wide, aux = factor_ref.shape[0], metric_ref.shape[0]
    chip, core = position()
    row = lax.broadcasted_iota(jnp.int32, (wide, aux), 0) // GROUP
    column = lax.broadcasted_iota(jnp.int32, (wide, aux), 1)
    pick = (row == column).astype(jnp.bfloat16)
    place = row // 2
    far = jnp.where(place < 2, 0, lax.bitwise_and(place, 1))
    away = jnp.where(place < 2, place, lax.bitwise_xor(place, core))
    origin = 2 * lax.bitwise_xor(away, chip) + lax.bitwise_xor(lax.bitwise_xor(lax.bitwise_and(row, 1), far), core)
    pick_origin = (origin == column).astype(jnp.bfloat16)
    tall = jnp.dot(pick, metric_ref[...], preferred_element_type=jnp.float32).astype(jnp.bfloat16)
    spread = lax.dot_general(tall, pick_origin, (((1,), (1,)), ((), ())), preferred_element_type=jnp.float32)
    same = lax.rem(lax.broadcasted_iota(jnp.int32, (wide, wide), 0), GROUP) == lax.rem(
        lax.broadcasted_iota(jnp.int32, (wide, wide), 1), GROUP
    )
    factor_ref[...] = jnp.where(same, spread, 0.0).astype(jnp.bfloat16)


def place_blocks(small_ref, held):
    for o in range(held.shape[0]):
        held[small_ref[0, o]] = o


def served(k, f, chip, core):
    there = lax.bitwise_xor(chip, 2 * k + core)
    return 2 * there + (core if f == 0 else 1 - core)


def early_kernel(hops, small_ref, raw_ref, *refs):
    *outs, held = refs
    place_blocks(small_ref, held)
    blocks, tile = raw_ref.shape[0], raw_ref.shape[2]
    chip, core = position()
    lane = lax.broadcasted_iota(jnp.int32, (tile, 128), 1)
    mine = jnp.zeros((tile, 128), jnp.int32)
    for n in range(4):
        mine = jnp.where(lane == n, small_ref[0:1, blocks + n : blocks + n + 1], mine)
    mine = mine.astype(jnp.float32).astype(jnp.bfloat16)
    for k, out in zip(hops, outs):
        if k > 0:
            for f in range(2):
                for w in range(2):
                    block = held[2 * served(k, f, chip, core) + w]
                    for s in range(EARLY):
                        out[(f * 2 + w) * EARLY + s] = raw_ref[block, s]
        if out.shape[0] % 2:
            out[out.shape[0] - 1] = mine


def counts_kernel(*refs):
    *got, out = refs
    for n, ref in enumerate(got):
        out[n : n + 1, :] = ref[ref.shape[0] - 1, 0:16, :].astype(jnp.float32)[0:1, :].astype(jnp.int32)


def late_kernel(hops, small_ref, counts_ref, crossed_ref, own_raw, peer_raw, *refs):
    outs = refs[: len(hops)]
    held, table = refs[-2:]
    blocks, slots = own_raw.shape[0], own_raw.shape[1] + 1
    half = counts_ref.shape[0]
    chip, core = position()
    place_blocks(small_ref, held)
    for line in range(4):
        for k in range(half):
            table[4 * k + line] = counts_ref[k, line]
            table[4 * (half + k) + line] = crossed_ref[k, line]
        table[8 * half + line] = small_ref[0, blocks + line]

    def live(block):
        m = lax.bitwise_xor(block // 4, chip)
        far = lax.bitwise_and(lax.bitwise_xor(m, core), 1)
        sender = jnp.where(m >= 2, lax.bitwise_xor(core, far), core)
        line = 2 * lax.bitwise_xor(lax.bitwise_and(block // 2, 1), sender) + lax.bitwise_and(block, 1)
        row = jnp.where(m < 2, jnp.where(m == 0, 2 * half, 0), m // 2 + half * far)
        return table[4 * row + line]

    def fill(target, at, raw, first, second, count, start):
        for j in range(slots - start if start == 0 else slots - 1 - start):
            from_first = j + start < count
            block = jnp.where(from_first, first, second)
            slot = jnp.where(from_first, j + start, (slots - 1 if start == 0 else slots - 2) - j)
            target[at + j] = raw[block, slot]

    def send(dest, target, own_start, peer_start):
        first, second = held[2 * dest], held[2 * dest + 1]
        count = live(first)
        fill(target, 0, own_raw, first, second, count, own_start)
        fill(target, slots - 1 - own_start if own_start else slots, peer_raw, first, second, count, peer_start)
        return count, second

    for k, out in zip(hops, outs):
        if k > 0:
            for f in range(2):
                send(served(k, f, chip, core), out.at[f], EARLY, EARLY if k > 1 else 0)
        else:
            self_ref, info_ref = refs[len(hops) : len(hops) + 2]
            send(2 * lax.bitwise_xor(chip, 1) + core, out, 0, 0)
            count, second = send(2 * chip + core, self_ref, 0, 0)
            row = lax.broadcasted_iota(jnp.int32, info_ref.shape, 0)
            info_ref[...] = jnp.where(row == 0, count, live(second))


def cross_kernel(*refs):
    *got, out = refs
    at = 0
    for ref in got:
        late = len(ref.shape) == 4
        tiles = ref.shape[1] if late else 2 * EARLY
        out[at : at + tiles] = ref[1] if late else ref[2 * EARLY : 4 * EARLY]
        at += tiles


def blank_kernel(out_ref, zeros, sem):
    zeros[...] = jnp.zeros_like(zeros)
    height = zeros.shape[0]
    copies = [
        pltpu.make_async_copy(zeros, out_ref.at[which, n * height : (n + 1) * height], sem.at[which, n])
        for which in range(2)
        for n in range(out_ref.shape[1] // height)
    ]
    for copy in copies:
        copy.start()
    for copy in copies:
        copy.wait()


def exchange_kernel(chips, blank_ref, info_ref, factor_ref, self_ref, side_ref, *refs):
    half = chips // 2
    first, refs = refs[: half - 1], refs[half - 1 :]
    second, refs = (None, *refs[: half - 2]), refs[half - 2 :]
    third, crossed, refs = refs[: half - 1], refs[half - 1], refs[half:]
    out_ref, rows, stage, sems = refs
    doubled, orbitals, width = self_ref.shape
    slots = doubled // 2
    wide = factor_ref.shape[0]
    first_live = info_ref[0:1, :]

    def choose(s, early, late, at):
        mirror = slots - 1 - s
        ours = early(s) if s < EARLY else late(s - EARLY) if s < slots - 1 else None
        theirs = early(EARLY + mirror) if mirror < EARLY else late(slots - 2 - mirror) if mirror < slots - 1 else None
        if ours is None or theirs is None:
            return theirs if ours is None else ours
        return jnp.where(first_live > s, ours.astype(jnp.float32), theirs.astype(jnp.float32)).astype(ours.dtype)

    def pieces(s, start):
        at = slice(start, start + GROUP)
        found = []
        for ref in (self_ref, side_ref):
            found += [ref[q * slots + s, at, :] for q in range(2)]
        own_late = slots - 1 - EARLY
        for k in range(1, half):
            for f in range(2):
                tiles = third[k - 1].shape[1]
                skip = (2 * half - 3) * 2 * EARLY + sum(ref.shape[1] for ref in third[: k - 1])
                late_ref = crossed.at[skip : skip + tiles] if f else third[k - 1].at[0]
                for q in range(2):
                    base = q * own_late
                    if q == 1 and k == 1:
                        found.append(late_ref[base + s, at, :])
                        continue
                    if f == 0:
                        early_ref, early_base = (first, second)[q][k - 1], 0
                    else:
                        early_ref, early_base = crossed, 2 * EARLY * (k - 1 + q * (half - 2))
                    found.append(
                        choose(
                            s,
                            lambda n, ref=early_ref, base=early_base: ref[base + n, at, :],
                            lambda n, ref=late_ref, base=base: ref[base + n, at, :],
                            at,
                        )
                    )
        return jnp.concatenate(found, axis=0)

    def span(n):
        return slice(n * width, (n + 1) * width)

    for part in range(orbitals // GROUP):
        columns = [pieces(s, part * GROUP) for s in range(slots)]
        fitted = jnp.dot(factor_ref[...], jnp.concatenate(columns, axis=1), preferred_element_type=jnp.float32)
        rows[part * wide : (part + 1) * wide, :] = fitted.astype(jnp.bfloat16)

    live = [info_ref[which, 0] for which in range(2)]

    def tiles(s, act):
        for which in range(2):
            row = s if which == 0 else slots - 1 - s
            for t in range(slots):
                column = t if which == 0 else slots - 1 - t
                if max(row, column) < slots - 1:

                    @pl.when(max(row, column) < live[which])
                    def _(which=which, row=row, column=column, t=t):
                        act(
                            pltpu.make_async_copy(
                                stage.at[span(s), span(t)],
                                out_ref.at[which, span(row), span(column)],
                                sems.at[which, row],
                            )
                        )

    for group in [range(n, n + 2) for n in range(0, slots, 2)]:
        for s in group:
            stage[span(s), :] = lax.dot_general(
                rows[:, span(s)], rows[...], (((0,), (0,)), ((), ())), preferred_element_type=jnp.float32
            )
        for s in group:
            tiles(s, lambda copy: copy.start())
    for s in range(slots):
        tiles(s, lambda copy: copy.wait())


def shards(devices, raw_tiles, metric, owner_map, counts):
    chips = devices // 2
    half = chips // 2
    _, blocks, orbitals, slots, width = raw_tiles.shape
    lines = -(-(blocks + 4) // 128) * 128
    raw = raw_tiles[0].transpose(0, 2, 1, 3)
    tie = lax.optimization_barrier

    def swap(x):
        return lax.ppermute(x, "aux", [(i, i ^ 1) for i in range(devices)])

    def hop(x, k):
        def target(i):
            away = 1 if k == 0 else 2 * k + i % 2
            return (i // 2 ^ away) * 2 + i % 2

        return lax.ppermute(x, "aux", [(i, target(i)) for i in range(devices)])

    def shape(*dims):
        return jax.ShapeDtypeStruct(dims, raw.dtype)

    other, raw = tie((swap(counts), raw[:, : slots - 1]))
    small = jnp.concatenate([owner_map, counts, other, jnp.zeros((lines - blocks - 4,), jnp.int32)]).reshape(1, lines)

    far = [*reversed(range(2, half))]
    near = [1, 0]
    place = pltpu.SMEM((blocks,), jnp.int32)

    def early(hops, raw, counted):
        return pl.pallas_call(
            functools.partial(early_kernel, hops),
            out_shape=[shape((4 * EARLY if k else 0) + counted, orbitals, width) for k in hops],
            in_specs=[VMEM] * 2,
            out_specs=[VMEM] * len(hops),
            scratch_shapes=[place],
            compiler_params=LIMIT,
            name="early",
        )(small, raw)

    def hops(ks, xs):
        return [hop(x, k) for k, x in zip(ks, xs)]

    ways = far + near
    first, raw_there = tie((early(ways, raw, 1), raw))
    factor = pl.pallas_call(
        factor_kernel,
        out_shape=shape(devices * GROUP, devices * GROUP),
        in_specs=[VMEM],
        out_specs=VMEM,
        compiler_params=LIMIT,
        name="factor",
    )(metric)
    peer_raw, factor = tie((swap(raw_there), factor))
    first = hops(ways, first)
    second = hops(far, early(far, peer_raw, 0))
    *first, beside, side = tie(first)
    first = [side, beside, *first[::-1]]
    brought = pl.pallas_call(
        counts_kernel,
        out_shape=jax.ShapeDtypeStruct((half, 128), jnp.int32),
        in_specs=[VMEM] * half,
        out_specs=VMEM,
        compiler_params=LIMIT,
        name="counts",
    )(*first)
    brought_there = swap(brought)

    def late(ks, small, extra=()):
        own = slots - 1 - EARLY
        tiles = [own + (own if k > 1 else slots) for k in ks]
        out_shape = [shape(2, n, orbitals, width) if k else shape(2 * slots, orbitals, width) for k, n in zip(ks, tiles)]
        out_shape += extra
        return pl.pallas_call(
            functools.partial(late_kernel, ks),
            out_shape=out_shape,
            in_specs=[VMEM] * 5,
            out_specs=[VMEM] * len(out_shape),
            scratch_shapes=[place, pltpu.SMEM((8 * half + 4,), jnp.int32)],
            compiler_params=LIMIT,
            cost_estimate=pl.CostEstimate(flops=0, bytes_accessed=1024, transcendentals=0),
            name="late",
        )(small, brought, brought_there, raw, peer_raw)

    *third, own, info = late(
        far + near, small, [shape(2 * slots, orbitals, width), jax.ShapeDtypeStruct((8, 128), jnp.int32)]
    )
    pairs = [tie((x, y)) for x, y in zip(third[: len(far)], second[::-1])]
    third = [x for x, _ in pairs] + third[len(pairs) :]
    second = [y for _, y in pairs][::-1]
    own_tiles = own
    blank = pl.pallas_call(
        lambda _, *refs: blank_kernel(*refs),
        out_shape=jax.ShapeDtypeStruct((2, slots * width, slots * width), jnp.float32),
        in_specs=[HBM],
        out_specs=HBM,
        scratch_shapes=[pltpu.VMEM((width, slots * width), jnp.float32), pltpu.SemaphoreType.DMA((2, slots))],
        compiler_params=LIMIT,
        name="blank",
    )(info)
    *third, blank = tie(hops(far + near, third) + [blank])
    third = third[::-1]
    second = second[::-1]
    crossed = pl.pallas_call(
        cross_kernel,
        out_shape=shape((2 * half - 3) * 2 * EARLY + sum(x.shape[1] for x in third[1:]), orbitals, width),
        in_specs=[VMEM] * (3 * half - 4),
        out_specs=VMEM,
        compiler_params=LIMIT,
        name="cross",
    )(*first[1:], *second, *third[1:])
    crossed = swap(crossed)

    return pl.pallas_call(
        functools.partial(exchange_kernel, chips),
        out_shape=jax.ShapeDtypeStruct((2, slots * width, slots * width), jnp.float32),
        in_specs=[HBM] + [VMEM] * (3 * half + 1),
        out_specs=HBM,
        scratch_shapes=[
            pltpu.VMEM((devices * orbitals, slots * width), raw.dtype),
            pltpu.VMEM((slots * width, slots * width), jnp.float32),
            pltpu.SemaphoreType.DMA((2, slots)),
        ],
        input_output_aliases={0: 0},
        compiler_params=pltpu.CompilerParams(vmem_limit_bytes=32 * 1024 * 1024),
        name="exchange",
    )(blank, info, factor, own_tiles, third[0], *first[1:], *second, *third[1:], crossed)


def solution(mesh):
    in_specs = (
        P(("grp", "aux"), None, None, None, None),
        P("grp", None),
        P("grp"),
        P(("grp", "aux")),
    )
    out_specs = P(("grp", "aux"), None, None)
    body = functools.partial(shards, mesh.shape["aux"])
    return jax.shard_map(body, mesh=mesh, in_specs=in_specs, out_specs=out_specs, check_vma=False)
```
